512 devices in a mesh: row: 8 (over x, core), col: 4 (over y), gz: 16 (over z).
Axes of the slice: x: 4, y: 4, z: 16, core: 2. Of those that a mesh axis runs over, the one named last changes fastest.
Arguments:
- parent: int32 [64], P('gz'), may hold values from 0 to 3, as said below
- l_tree: bfloat16 [64, 256, 256], P('gz', 'row', 'col'), may hold values from -0.375 to 0.375
- l_path: bfloat16 [128, 4, 256, 256], P('gz', None, 'row', 'col'), may hold values from -0.09375 to 0.09375
- l_top: bfloat16 [15, 4, 256, 256], P(None, None, 'row', 'col'), may hold values from -0.25 to 0.25
- u_tree: bfloat16 [64, 256, 256], P('gz', 'col', 'row'), may hold values from -0.375 to 0.375
- u_path: bfloat16 [128, 4, 256, 256], P('gz', None, 'col', 'row'), may hold values from -0.1875 to 0.1875
- u_top: bfloat16 [15, 4, 256, 256], P(None, None, 'col', 'row'), may hold values from -0.1875 to 0.1875
- linv_local: bfloat16 [128, 256, 256], P('gz', 'col'), may hold values from -0.375 to 0.375
- linv_top: bfloat16 [15, 256, 256], P(None, 'col'), may hold values from -0.375 to 0.375
- uinv_local: bfloat16 [128, 256, 256], P('gz', 'row'), may hold values from -0.375 to 0.375
- uinv_top: bfloat16 [15, 256, 256], P(None, 'row'), may hold values from -0.375 to 0.375
- rhs_local: bfloat16 [128, 256, 512], P('gz', 'row'), may hold values from -6 to 6
- rhs_top: bfloat16 [15, 256, 512], P(None, 'row'), may hold values from -6 to 6
Outputs:
- x_local: float32 [128, 256, 512], P('gz', ('row', 'col'))
- x_path: float32 [16, 4, 256, 512], P('gz', None, ('row', 'col'))
The draws below stay inside these ranges and needn't reach their ends.
Inputs may be any that keep to these rules, and one draw needn't show every extreme that they name: Entry g * 4 + j names, within layer g, the level-one parent of level-zero supernode j; in every layer some supernode has parent 0 and some has parent 4 - 1.
All inputs are finite; a program needn't handle non-finite values.
Results may differ from the reference program's by a relative error of at most 0.04.
Values may be sent and summed in bfloat16 or wider, within the bound.
A program may use at most 64 MiB of HBM per device.

```python
import jax
import jax.numpy as jnp
import numpy as np

W = 256
R = 512
NPL = 4
LOC = 8
TOPL = 4
NA = 15
LEAFS = 64
NLOC = 128
N_GZ = 16


def draw_parent(key, part):
    key = jax.random.fold_in(key, 7)
    layer_keys = jax.random.split(key, LEAFS // NPL)
    orders = jax.vmap(lambda inner: jax.random.permutation(inner, NPL))(layer_keys).reshape(-1)
    low_one = jax.random.randint(jax.random.fold_in(key, 1), (LEAFS,), 0, NPL, dtype=jnp.int32)
    low_two = jax.random.randint(jax.random.fold_in(key, 2), (LEAFS,), 0, NPL, dtype=jnp.int32)
    keeper = (orders == 0) | (orders == NPL - 1)
    return jnp.where(keeper, orders.astype(jnp.int32), jnp.minimum(low_one, low_two)).astype(jnp.int32)


def block_scale(rng, dims, shards, smallest, largest):
    level, own = 1.0, jax.random.fold_in(rng, 6)
    for dim, blocks in shards:
        steps = jnp.exp(jax.random.uniform(jax.random.fold_in(own, dim), (blocks,), jnp.float32, smallest / len(shards), largest / len(shards)))
        level = level * jnp.repeat(steps, dims[dim] // blocks).reshape([-1 if axis == dim else 1 for axis in range(len(dims))])
    return level


def centred(rng, dims, spread, limit, cuts=(), kind=jnp.bfloat16):
    result = spread * jax.random.normal(rng, dims, jnp.float32)
    if cuts:
        result = result * block_scale(rng, dims, cuts, -0.22, 0.18)
    return jnp.clip(result, -limit, limit).astype(kind)


def setup_inputs(seed: int = 0) -> dict:
    splits = jax.random.split(jax.random.key(seed), 14)
    return {
        "parent": draw_parent(jax.random.fold_in(splits[13], 71), 0),
        "l_tree": centred(splits[1], (LEAFS, W, W), W ** -0.5, 0.375, ((0, 16), (1, 8), (2, 4))),
        "l_path": centred(splits[2], (NLOC, TOPL, W, W), (2 * W * LOC) ** -0.5, 0.09375, ((0, 16), (2, 8), (3, 4))),
        "l_top": centred(splits[3], (NA, TOPL, W, W), (2 * W) ** -0.5, 0.25, ((2, 8), (3, 4))),
        "u_tree": centred(splits[4], (LEAFS, W, W), W ** -0.5, 0.375, ((0, 16), (1, 4), (2, 8))),
        "u_path": centred(splits[5], (NLOC, TOPL, W, W), (W * TOPL) ** -0.5, 0.1875, ((0, 16), (2, 4), (3, 8))),
        "u_top": centred(splits[6], (NA, TOPL, W, W), (W * TOPL) ** -0.5, 0.1875, ((2, 4), (3, 8))),
        "linv_local": centred(splits[7], (NLOC, W, W), W ** -0.5, 0.375, ((0, 16), (1, 4))),
        "linv_top": centred(splits[8], (NA, W, W), W ** -0.5, 0.375, ((1, 4),)),
        "uinv_local": centred(splits[9], (NLOC, W, W), W ** -0.5, 0.375, ((0, 16), (1, 8))),
        "uinv_top": centred(splits[10], (NA, W, W), W ** -0.5, 0.375, ((1, 8),)),
        "rhs_local": centred(splits[11], (NLOC, W, R), 1.0, 6.0, ((0, 16), (1, 8))),
        "rhs_top": centred(splits[12], (NA, W, R), 1.0, 6.0, ((1, 8),)),
    }


def batched(blocks, vectors, einsum_form):
    return jnp.einsum(einsum_form, blocks.astype(jnp.float32), vectors.astype(jnp.float32))


def ancestor_table():
    path_table = np.zeros((N_GZ, TOPL), np.int32)
    for layer_id in range(N_GZ):
        for tree_level in range(TOPL):
            path_table[layer_id, tree_level] = N_GZ - (N_GZ >> tree_level) + (layer_id >> (tree_level + 1))
    return path_table


def reference(parent, l_tree, l_path, l_top, u_tree, u_path, u_top, linv_local, linv_top, uinv_local, uinv_top, rhs_local, rhs_top):
    path_table = ancestor_table()
    single_form = "gkab,gkbr->gkar"
    node_form = "nab,nbr->nar"
    linv_layers = linv_local.reshape(N_GZ, LOC, W, W)
    upper_inverse_layers = uinv_local.reshape(N_GZ, LOC, W, W)
    rhs_layers = rhs_local.reshape(N_GZ, LOC, W, R)
    lpath_layers = l_path.reshape(N_GZ, LOC, TOPL, W, W)
    upath_layers = u_path.reshape(N_GZ, LOC, TOPL, W, W)
    ltree_layers = l_tree.reshape(N_GZ, NPL, W, W)
    utree_layers = u_tree.reshape(N_GZ, NPL, W, W)
    parents = parent.reshape(N_GZ, NPL)
    select_option = (parents[:, :, None] == jnp.arange(NPL, dtype=jnp.int32)[None, None, :]).astype(jnp.float32)

    first_y = batched(linv_layers[:, :NPL], rhs_layers[:, :NPL], single_form)
    first_low = first_y.astype(jnp.bfloat16)
    forwarded_values = jnp.einsum("gji,gjar->giar", select_option, batched(ltree_layers, first_low, single_form))
    second_rhs = (rhs_layers[:, NPL:].astype(jnp.float32) - forwarded_values).astype(jnp.bfloat16)
    second_y = batched(linv_layers[:, NPL:], second_rhs, single_form)
    local_low = jnp.concatenate([first_y, second_y], 1).astype(jnp.bfloat16)
    toward = batched(lpath_layers, local_low, "gkmab,gkbr->gmar")
    pending = jnp.zeros((NA, W, R), jnp.float32)
    for tree_level in range(TOPL):
        pending = pending.at[path_table[:, tree_level]].add(toward[:, tree_level])

    top_y = jnp.zeros((NA, W, R), jnp.float32)
    for tree_level in range(TOPL):
        span_start = N_GZ - (N_GZ >> tree_level)
        extent_count = N_GZ >> (tree_level + 1)
        node_span = slice(span_start, span_start + extent_count)
        upper_right_hand = (rhs_top[node_span].astype(jnp.float32) - pending[node_span]).astype(jnp.bfloat16)
        solved = batched(linv_top[node_span], upper_right_hand, node_form)
        top_y = top_y.at[node_span].set(solved)
        solved_low = solved.astype(jnp.bfloat16)
        for upper_level in range(tree_level + 1, TOPL):
            targets = N_GZ - (N_GZ >> upper_level) + (np.arange(extent_count) >> (upper_level - tree_level))
            pending = pending.at[targets].add(batched(l_top[node_span, upper_level], solved_low, node_form))

    top_x = jnp.zeros((NA, W, R), jnp.float32)
    for tree_level in reversed(range(TOPL)):
        span_start = N_GZ - (N_GZ >> tree_level)
        extent_count = N_GZ >> (tree_level + 1)
        node_span = slice(span_start, span_start + extent_count)
        update = jnp.zeros((extent_count, W, R), jnp.float32)
        for upper_level in range(tree_level + 1, TOPL):
            targets = N_GZ - (N_GZ >> upper_level) + (np.arange(extent_count) >> (upper_level - tree_level))
            update = update + batched(u_top[node_span, upper_level], top_x[targets].astype(jnp.bfloat16), node_form)
        top_s = (top_y[node_span] - update).astype(jnp.bfloat16)
        top_x = top_x.at[node_span].set(batched(uinv_top[node_span], top_s, node_form))

    path_low = top_x.astype(jnp.bfloat16)[path_table]
    path_term = batched(upath_layers, path_low, "gkmab,gmbr->gkar")
    second_s = (second_y - path_term[:, NPL:]).astype(jnp.bfloat16)
    second_x = batched(upper_inverse_layers[:, NPL:], second_s, single_form)
    parent_low = jnp.einsum("gji,giar->gjar", select_option, second_x.astype(jnp.bfloat16).astype(jnp.float32))
    tree_term = batched(utree_layers, parent_low, single_form)
    first_s = (first_y - path_term[:, :NPL] - tree_term).astype(jnp.bfloat16)
    first_x = batched(upper_inverse_layers[:, :NPL], first_s, single_form)
    x_local = jnp.concatenate([first_x, second_x], 1).reshape(NLOC, W, R)
    x_path = top_x[path_table]
    return x_local, x_path
```

```python
import functools

import jax
import jax.numpy as jnp
from jax import lax
from jax.experimental import pallas as pl
from jax.experimental.pallas import tpu as pltpu
from jax.sharding import PartitionSpec as P

F32 = jnp.float32
BF16 = jnp.bfloat16
MESH = pl.DeviceIdType.MESH
ROWS, COLS, LAYERS = 8, 4, 16
NPL, LOC, TOPL = 4, 8, 4
W, R = 256, 512
SLAB, KCH = W // ROWS, W // COLS
CG = R // COLS
CP = CG // ROWS
L_PAIRS = ((0, 1), (0, 2), (0, 3), (1, 2), (1, 3), (2, 3))
Z_BASE = (0, 4, 7, 9)


def nt(a, b):
    return lax.dot_general(a, b, (((1,), (1,)), ((), ())), preferred_element_type=F32)


def mm(a, b):
    return jnp.dot(a, b, preferred_element_type=F32)


def aligned(value, size):
    return pl.ds(pl.multiple_of(value * size, size), size)


def kernel(
    parent, l_tree, l_path, l_top, u_tree, u_path, u_top, linv_local, linv_top, uinv_local,
    uinv_top, rhs_local, rhs_top, x_local, x_path,
    st_ltree, st_lpath, st_ltop, st_utree, st_upath, st_utop, uinv_own, rhs2_own, st_rt,
    x1, linv, lt, lp, ltp1, ltp, linvt, uinvt, uinv2, up, us, ut,
    y, ylow, s2f, tt, rv, rt, rr, zs, zr, xp, sb2, x2low, sb1, out_l, out_p,
    lsem, ssem, rsem,
):
    r = lax.axis_index("row")
    c = lax.axis_index("col")
    g = lax.axis_index("gz")
    counters = {"l": 0, "s": 0, "r": 0}
    pending_sends = []

    def take(kind, count=1):
        first = counters[kind]
        counters[kind] += count
        return first

    def local(src, dst):
        copy = pltpu.make_async_copy(src, dst, lsem.at[take("l")])
        copy.start()
        return copy

    def remote(src, dst, slot, target):
        copy = pltpu.make_async_remote_copy(
            src_ref=src, dst_ref=dst, send_sem=ssem.at[take("s")], recv_sem=rsem.at[slot],
            device_id=target, device_id_type=MESH,
        )
        copy.start()
        pending_sends.append(copy)

    def await_slot(dst, slot):
        pltpu.make_async_remote_copy(
            src_ref=dst, dst_ref=dst, send_sem=ssem.at[0], recv_sem=rsem.at[slot],
            device_id={"row": r}, device_id_type=MESH,
        ).wait_recv()

    def spread(axis, src_of, dst_of):
        me, size = (r, ROWS) if axis == "row" else (c, COLS)
        base = take("r", size)
        for step in range(1, size):
            peer = lax.rem(me + step, size)
            remote(src_of(peer), dst_of(me), base + step, {axis: peer})

        def wait():
            for step in range(1, size):
                await_slot(dst_of(lax.rem(me + size - step, size)), base + step)

        return wait

    anc = [LAYERS - (LAYERS >> a) + g // 2 ** (a + 1) for a in range(TOPL)]
    my_rows = aligned(r, SLAB)
    my_k = aligned(c, KCH)
    my_cols = aligned(c, CG)

    barrier = pltpu.get_barrier_semaphore()
    for step in range(1, ROWS):
        pl.semaphore_signal(barrier, inc=1, device_id={"row": lax.rem(r + step, ROWS)}, device_id_type=MESH)
    for step in range(1, COLS):
        pl.semaphore_signal(barrier, inc=1, device_id={"col": lax.rem(c + step, COLS)}, device_id_type=MESH)
    partners = []
    for a in range(TOPL):
        span = 2**a
        partners.append(g + span - 2 * span * lax.rem(g // span, 2))
        pl.semaphore_signal(barrier, inc=1, device_id={"gz": partners[a]}, device_id_type=MESH)

    c_ltree = local(l_tree, st_ltree)
    c_lpath = local(l_path, st_lpath)
    c_ltop = [local(l_top.at[anc[a]], st_ltop.at[a]) for a in range(3)]
    c_rt = [local(rhs_top.at[anc[a], :, my_cols], st_rt.at[a]) for a in range(TOPL)]
    c_x1 = local(rhs_local.at[pl.ds(0, NPL), :, my_cols], x1.at[:, my_rows, :])
    c_li1 = local(linv_local.at[pl.ds(0, NPL)], linv.at[pl.ds(0, NPL), my_k, :])
    c_li2 = local(linv_local.at[pl.ds(NPL, NPL)], linv.at[pl.ds(NPL, NPL), my_k, :])
    c_lit = [local(linv_top.at[anc[a]], linvt.at[a, my_k, :]) for a in range(TOPL)]
    c_rhs2 = local(rhs_local.at[pl.ds(NPL, NPL), :, my_cols], rhs2_own)
    c_utree = local(u_tree, st_utree)
    c_upath = local(u_path, st_upath)
    c_utop = [local(u_top.at[anc[a]], st_utop.at[a]) for a in range(3)]
    c_uiown = local(uinv_local, uinv_own)
    c_ui2 = local(uinv_local.at[pl.ds(NPL, NPL)], uinv2.at[:, my_rows, :])
    c_uit = [local(uinv_top.at[anc[a]], uinvt.at[a, my_rows, :]) for a in range(TOPL)]

    pl.semaphore_wait(barrier, ROWS - 1 + COLS - 1 + TOPL)

    w_x1 = spread(
        "row", lambda peer: rhs_local.at[pl.ds(0, NPL), :, my_cols],
        lambda me: x1.at[:, aligned(me, SLAB), :],
    )
    w_li1 = spread(
        "col", lambda peer: linv_local.at[pl.ds(0, NPL)],
        lambda me: linv.at[pl.ds(0, NPL), aligned(me, KCH), :],
    )
    odd = lax.rem(c, 2)

    def shifted(block):
        blank = jnp.zeros_like(block)
        low = jnp.concatenate([block, blank], axis=-1)
        high = jnp.concatenate([blank, block], axis=-1)
        return jnp.where(odd == 0, low, high)

    c_ltree.wait()
    for j in range(NPL):
        lt[c, j] = shifted(st_ltree[j])
    w_lt = spread("col", lambda peer: lt.at[c], lambda me: lt.at[me])
    w_li2 = spread(
        "col", lambda peer: linv_local.at[pl.ds(NPL, NPL)],
        lambda me: linv.at[pl.ds(NPL, NPL), aligned(me, KCH), :],
    )
    c_lpath.wait()
    for m in range(TOPL):
        lp[c, pl.ds(m * SLAB, SLAB), :] = jnp.concatenate([st_lpath[k, m] for k in range(LOC)], axis=-1)
    w_lp = spread("col", lambda peer: lp.at[c], lambda me: lp.at[me])
    for copy in c_ltop:
        copy.wait()
    for b, (a, m) in enumerate(L_PAIRS):
        ltp1[c, b] = shifted(st_ltop[a, m])
    w_ltp1 = spread("col", lambda peer: ltp1.at[c], lambda me: ltp1.at[me])
    for copy in c_lit:
        copy.wait()
    w_lit = spread("col", lambda peer: linvt.at[:, my_k, :], lambda me: linvt.at[:, aligned(me, KCH), :])

    eye = (
        lax.broadcasted_iota(jnp.int32, (CG, CG), 0) == lax.broadcasted_iota(jnp.int32, (CG, CG), 1)
    ).astype(F32).astype(BF16)
    for copy in c_rt:
        copy.wait()
    rt[...] = nt(eye, st_rt[...].reshape(TOPL * SLAB, CG)).astype(BF16)
    w_rr = spread("row", lambda peer: rt.at[aligned(peer, CP), :], lambda me: rr.at[me])
    rr[r] = rt[aligned(r, CP), :]

    eye_k = eye[0:KCH, 0:KCH]

    def packed(stack):
        return nt(eye_k, stack).astype(BF16)

    c_upath.wait()
    for k in range(LOC):
        up[k, my_k, :] = packed(st_upath[k].reshape(CG, KCH))
    c_utree.wait()
    up[LOC, my_k, :] = packed(st_utree[...].reshape(CG, KCH))
    for copy in c_utop:
        copy.wait()
    up[LOC + 1, my_k, :] = packed(jnp.concatenate([st_utop[2, 3], st_utop[0, 1], st_utop[0, 2], st_utop[0, 3]], axis=0))
    up[LOC + 2, my_k, :] = packed(st_utop[1].reshape(CG, KCH))

    c_x1.wait()
    c_li1.wait()
    w_x1()
    w_li1()
    for j in range(NPL):
        solved = mm(linv[j], x1[j])
        y[j] = solved
        ylow[j] = solved.astype(BF16)
    w_lt()
    terms = []
    for j in range(NPL):
        term = mm(lt[0, j] + lt[1, j], ylow[j, 0:CG, :]) + mm(lt[2, j] + lt[3, j], ylow[j, CG:W, :])
        terms.append(term)
    c_rhs2.wait()
    for i in range(NPL):
        value = rhs2_own[i].astype(F32)
        for j in range(NPL):
            value = value - jnp.where(parent[j] == i, 1.0, 0.0).astype(F32) * terms[j]
        s2f[i, my_rows, :] = value.astype(BF16)
    w_s2 = spread("row", lambda peer: s2f.at[:, my_rows, :], lambda me: s2f.at[:, aligned(me, SLAB), :])

    w_up = spread("col", lambda peer: up.at[:, my_k, :], lambda me: up.at[:, aligned(me, KCH), :])
    w_ltp1()
    for b in range(len(L_PAIRS)):
        ltp[b, my_rows, :] = jnp.concatenate([ltp1[0, b] + ltp1[1, b], ltp1[2, b] + ltp1[3, b]], axis=-1)
    w_ltp = spread("row", lambda peer: ltp.at[:, my_rows, :], lambda me: ltp.at[:, aligned(me, SLAB), :])
    for copy in c_uit:
        copy.wait()

    w_lp()
    toward = jnp.zeros((TOPL * SLAB, CG), F32)
    for q in range(COLS):
        block = ylow[0:NPL, q * KCH:(q + 1) * KCH, :].reshape(NPL * KCH, CG)
        toward = toward + mm(lp[q, :, 0:NPL * KCH], block)

    c_li2.wait()
    w_li2()
    w_s2()
    for i in range(NPL):
        solved = mm(linv[NPL + i], s2f[i])
        y[NPL + i] = solved
        ylow[NPL + i] = solved.astype(BF16)
    for q in range(COLS):
        block = ylow[NPL:LOC, q * KCH:(q + 1) * KCH, :].reshape(NPL * KCH, CG)
        toward = toward + mm(lp[q, :, NPL * KCH:LOC * KCH], block)
    tt[...] = nt(eye, toward.astype(BF16)).astype(BF16)
    w_rv = spread("row", lambda peer: tt.at[aligned(peer, CP), :], lambda me: rv.at[me])
    rv[r] = tt[aligned(r, CP), :]

    w_uit = spread("row", lambda peer: uinvt.at[:, my_rows, :], lambda me: uinvt.at[:, aligned(me, SLAB), :])

    slot_of_lane = lax.broadcasted_iota(jnp.int32, (CP, CG), 1) // SLAB

    def by_level(tiles, m):
        halves = []
        for q in range(2):
            total = None
            for s in range(4):
                piece = tiles[4 * q + s]
                if s != m:
                    piece = pltpu.roll(piece, (s - m) * SLAB % CG, 1)
                total = piece if total is None else jnp.where(slot_of_lane == s, piece, total)
            halves.append(total)
        return jnp.concatenate(halves, axis=-1)

    w_rr()
    rr_tiles = [rr[q].astype(F32) for q in range(ROWS)]
    top_rhs = [by_level(rr_tiles, m) for m in range(TOPL)]
    w_rv()
    rv_tiles = [rv[q].astype(F32) for q in range(ROWS)]
    pend = [by_level(rv_tiles, m) for m in range(TOPL)]

    top_y = []
    w_us = w_ut = None
    for a in range(TOPL):
        count = TOPL - a
        base = Z_BASE[a]
        for m in range(a, TOPL):
            zs[base + m - a] = pend[m].astype(BF16)
        slot = take("r")
        remote(zs.at[pl.ds(base, count)], zr.at[pl.ds(base, count)], slot, {"gz": partners[a]})
        if a == 0:
            c_ui2.wait()
            w_ui2 = spread("row", lambda peer: uinv2.at[:, my_rows, :], lambda me: uinv2.at[:, aligned(me, SLAB), :])
            w_up()
            u_lanes = pl.ds(pl.multiple_of(r * CG, CG), CG)
            w_ut = spread(
                "row", lambda peer: up.at[pl.ds(LOC + 1, 2)],
                lambda me: ut.at[:, :, pl.ds(pl.multiple_of(me * CG, CG), CG)],
            )
            w_us = spread(
                "row", lambda peer: up.at[pl.ds(0, LOC + 1), aligned(peer, SLAB), :],
                lambda me: us.at[:, :, pl.ds(pl.multiple_of(me * CG, CG), CG)],
            )
            c_ut = local(up.at[pl.ds(LOC + 1, 2)], ut.at[:, :, u_lanes])
            c_us = local(up.at[pl.ds(0, LOC + 1), my_rows, :], us.at[:, :, u_lanes])
            w_lit()
            w_ltp()
        await_slot(zr.at[pl.ds(base, count)], slot)
        for m in range(a, TOPL):
            pend[m] = pend[m] + zr[base + m - a].astype(F32)
        solved = nt((top_rhs[a] - pend[a]).astype(BF16), linvt[a])
        top_y.append(solved)
        low = solved.astype(BF16)
        for b, (source, m) in enumerate(L_PAIRS):
            if source == a:
                pend[m] = pend[m] + nt(low, ltp[b])

    c_ut.wait()
    w_ut()
    w_uit()
    tiles = [jnp.zeros((CP, CG), F32) for _ in range(ROWS)]
    for a in reversed(range(TOPL)):
        value = top_y[a]
        if a < TOPL - 1:
            if a == 2:
                known = [pltpu.roll(tile, SLAB, 1) for tile in tiles]
            else:
                known = tiles
            above = jnp.concatenate(known, axis=-1).astype(BF16)
            value = value - nt(above, ut[0 if a != 1 else 1])
        solved = nt(value.astype(BF16), uinvt[a])
        for q in range(2):
            half = solved[:, q * CG:(q + 1) * CG]
            for s in range(4):
                piece = half if a == s else pltpu.roll(half, (a - s) * SLAB % CG, 1)
                tiles[4 * q + s] = jnp.where(slot_of_lane == a, piece, tiles[4 * q + s])
    my_cp = aligned(r, CP)
    xp[my_cp, :] = jnp.concatenate(tiles, axis=-1).astype(BF16)
    w_xp = spread("row", lambda peer: xp.at[my_cp, :], lambda me: xp.at[aligned(me, CP), :])

    c_us.wait()
    w_us()
    w_xp()
    path = xp[...]
    path_term2 = nt(us[NPL:LOC].reshape(NPL * SLAB, ROWS * CG), path)
    for i in range(NPL):
        value = y[NPL + i, my_rows, :] - path_term2[i * SLAB:(i + 1) * SLAB, :]
        sb2[i, my_rows, :] = value.astype(BF16)
    w_sb2 = spread("row", lambda peer: sb2.at[:, my_rows, :], lambda me: sb2.at[:, aligned(me, SLAB), :])
    path_term1 = nt(us[0:NPL].reshape(NPL * SLAB, ROWS * CG), path)
    own_path = nt(eye, xp[:, pl.ds(pl.multiple_of(r * CG, CG), CG)])
    for m in range(TOPL):
        out_p[m] = own_path[m * SLAB:(m + 1) * SLAB, :]
    piece_rows = SLAB // COLS

    def out_rows(peer):
        return pl.ds(pl.multiple_of(peer * piece_rows, piece_rows), piece_rows)

    w_outp = spread(
        "col", lambda peer: out_p.at[:, out_rows(peer), :],
        lambda me: x_path.at[0, :, :, pl.ds(pl.multiple_of(me * CG, CG), CG)],
    )
    c_outp = local(out_p.at[:, out_rows(c), :], x_path.at[0, :, :, my_cols])
    lane_slot = lax.rem(lax.broadcasted_iota(jnp.int32, (SLAB, ROWS * CG), 1) // SLAB, NPL)
    tree_piece = us[LOC]
    tree_blocks = [jnp.where(lane_slot == j, tree_piece, jnp.zeros_like(tree_piece)) for j in range(NPL)]
    tree_weights = jnp.concatenate(tree_blocks, axis=0)

    w_ui2()
    c_uiown.wait()
    w_sb2()
    for i in range(NPL):
        x2low[i] = mm(uinv2[i], sb2[i]).astype(BF16)
    parent_x = [x2low[parent[j]].reshape(ROWS, 1, SLAB, CG) for j in range(NPL)]
    stacked = jnp.concatenate(parent_x, axis=1).reshape(ROWS * NPL * SLAB, CG)
    tree_term = mm(tree_weights, stacked)
    for j in range(NPL):
        rows = slice(j * SLAB, (j + 1) * SLAB)
        value = y[j, my_rows, :] - path_term1[rows, :] - tree_term[rows, :]
        sb1[j, my_rows, :] = value.astype(BF16)
    w_sb1 = spread("row", lambda peer: sb1.at[:, my_rows, :], lambda me: sb1.at[:, aligned(me, SLAB), :])
    for i in range(NPL):
        out_l[NPL + i] = mm(uinv_own[NPL + i], sb2[i])

    def send_out(first):
        part = pl.ds(first, NPL)
        wait = spread(
            "col", lambda peer: out_l.at[part, out_rows(peer), :],
            lambda me: x_local.at[part, :, pl.ds(pl.multiple_of(me * CG, CG), CG)],
        )
        return wait, local(out_l.at[part, out_rows(c), :], x_local.at[part, :, my_cols])

    w_out2, c_out2 = send_out(NPL)
    w_sb1()
    for j in range(NPL):
        out_l[j] = mm(uinv_own[j], sb1[j])
    w_out1, c_out1 = send_out(0)
    w_outp()
    w_out2()
    w_out1()
    for copy in (c_outp, c_out2, c_out1):
        copy.wait()
    for copy in pending_sends:
        copy.wait_send()


def per_device(*arrays):
    arrays = list(arrays)
    for index in (4, 5, 6):
        arrays[index] = jnp.swapaxes(arrays[index], -1, -2)
    any_space = pl.BlockSpec(memory_space=pl.ANY)
    vmem = pltpu.VMEM
    scratch = [
        vmem((NPL, SLAB, KCH), BF16),
        vmem((LOC, TOPL, SLAB, KCH), BF16),
        vmem((3, TOPL, SLAB, KCH), BF16),
        vmem((NPL, SLAB, KCH), BF16),
        vmem((LOC, TOPL, SLAB, KCH), BF16),
        vmem((3, TOPL, SLAB, KCH), BF16),
        vmem((LOC, SLAB, W), BF16),
        vmem((NPL, SLAB, CG), BF16),
        vmem((TOPL, SLAB, CG), BF16),
        vmem((NPL, W, CG), BF16),
        vmem((LOC, W, W), BF16),
        vmem((COLS, NPL, SLAB, CG), BF16),
        vmem((COLS, TOPL * SLAB, LOC * KCH), BF16),
        vmem((COLS, 6, SLAB, CG), BF16),
        vmem((6, W, W), BF16),
        vmem((TOPL, W, W), BF16),
        vmem((TOPL, W, W), BF16),
        vmem((NPL, W, W), BF16),
        vmem((LOC + 3, W, CG), BF16),
        vmem((LOC + 1, SLAB, ROWS * CG), BF16),
        vmem((2, W, ROWS * CG), BF16),
        vmem((LOC, W, CG), F32),
        vmem((LOC, W, CG), BF16),
        vmem((NPL, W, CG), BF16),
        vmem((CG, TOPL * SLAB), BF16),
        vmem((ROWS, CP, CG), BF16),
        vmem((CG, TOPL * SLAB), BF16),
        vmem((ROWS, CP, CG), BF16),
        vmem((10, CP, W), BF16),
        vmem((10, CP, W), BF16),
        vmem((CG, ROWS * CG), BF16),
        vmem((NPL, W, CG), BF16),
        vmem((NPL, W, CG), BF16),
        vmem((NPL, W, CG), BF16),
        vmem((LOC, SLAB, CG), F32),
        vmem((TOPL, SLAB, CG), F32),
        pltpu.SemaphoreType.DMA((48,)),
        pltpu.SemaphoreType.DMA((160,)),
        pltpu.SemaphoreType.DMA((160,)),
    ]
    return pl.pallas_call(
        kernel,
        out_shape=(
            jax.ShapeDtypeStruct((LOC, SLAB // COLS, R), F32),
            jax.ShapeDtypeStruct((1, TOPL, SLAB // COLS, R), F32),
        ),
        in_specs=[pl.BlockSpec(memory_space=pltpu.SMEM)] + [any_space] * 12,
        out_specs=(any_space, any_space),
        scratch_shapes=scratch,
        compiler_params=pltpu.CompilerParams(
            collective_id=0, has_side_effects=True, vmem_limit_bytes=60 * 1024 * 1024
        ),
    )(*arrays)


def solution(mesh):
    placed = (
        P("gz"),
        P("gz", "row", "col"),
        P("gz", None, "row", "col"),
        P(None, None, "row", "col"),
        P("gz", "col", "row"),
        P("gz", None, "col", "row"),
        P(None, None, "col", "row"),
        P("gz", "col", None),
        P(None, "col", None),
        P("gz", "row", None),
        P(None, "row", None),
        P("gz", "row", None),
        P(None, "row", None),
    )
    return jax.shard_map(
        per_device,
        mesh=mesh,
        in_specs=placed,
        out_specs=(P("gz", ("row", "col"), None), P("gz", None, ("row", "col"), None)),
        check_vma=False,
    )
```

```python
import functools

import jax
import jax.numpy as jnp
from jax import lax
from jax.experimental import pallas as pl
from jax.experimental.pallas import tpu as pltpu
from jax.sharding import PartitionSpec as P

F32 = jnp.float32
BF16 = jnp.bfloat16
MESH = pl.DeviceIdType.MESH
ROWS, COLS, LAYERS = 8, 4, 16
NPL, LOC, TOPL = 4, 8, 4
W, R = 256, 512
SLAB, KCH = W // ROWS, W // COLS
CG = R // COLS
CP = CG // ROWS
L_PAIRS = ((0, 1), (0, 2), (0, 3), (1, 2), (1, 3), (2, 3))
Z_BASE = (0, 4, 7, 9)


def nt(a, b):
    return lax.dot_general(a, b, (((1,), (1,)), ((), ())), preferred_element_type=F32)


def mm(a, b):
    return jnp.dot(a, b, preferred_element_type=F32)


def aligned(value, size):
    return pl.ds(pl.multiple_of(value * size, size), size)


def kernel(
    parent, l_tree, l_path, l_top, u_tree, u_path, u_top, linv_local, linv_top, uinv_local,
    uinv_top, rhs_local, rhs_top, x_local, x_path,
    st_ltree, st_lpath, st_ltop, st_utree, st_upath, st_utop, uinv_own, rhs2_own, st_rt,
    x1, linv, lt, lp, ltp1, ltp, linvt, uinvt, uinv2, up, us, utp, ut, tree_w,
    y, ylow, s2f, tt, rv, rt, rr, zs, zr, xp, sb2, x2low, sb1, out_l, out_p,
    lsem, ssem, rsem,
):
    r = lax.axis_index("row")
    c = lax.axis_index("col")
    g = lax.axis_index("gz")
    chip, core = r // 2, lax.rem(r, 2)
    sibling = chip * 2 + 1 - core
    counters = {"l": 0, "s": 0, "r": 0}
    pending_sends = []

    def take(kind, count=1):
        first = counters[kind]
        counters[kind] += count
        return first

    def local(src, dst):
        copy = pltpu.make_async_copy(src, dst, lsem.at[take("l")])
        copy.start()
        return copy

    def remote(src, dst, slot, target):
        copy = pltpu.make_async_remote_copy(
            src_ref=src, dst_ref=dst, send_sem=ssem.at[take("s")], recv_sem=rsem.at[slot],
            device_id=target, device_id_type=MESH,
        )
        copy.start()
        pending_sends.append(copy)

    def await_slot(dst, slot):
        pltpu.make_async_remote_copy(
            src_ref=dst, dst_ref=dst, send_sem=ssem.at[0], recv_sem=rsem.at[slot],
            device_id={"row": r}, device_id_type=MESH,
        ).wait_recv()

    def spread(axis, src_of, dst_of):
        me, size = (r, ROWS) if axis == "row" else (c, COLS)
        base = take("r", size)
        for step in range(1, size):
            peer = lax.rem(me + step, size)
            remote(src_of(peer), dst_of(me), base + step, {axis: peer})

        def wait():
            for step in range(1, size):
                await_slot(dst_of(lax.rem(me + size - step, size)), base + step)

        return wait

    def row_of(other_chip, other_core):
        return lax.rem(other_chip + 4, 4) * 2 + other_core

    def spread_row_shared(src, dst_of):
        base = take("r", 8)
        for step in range(1, 4):
            remote(src, dst_of(r), base + step, {"row": row_of(chip + step, core)})
        remote(src, dst_of(r), base, {"row": sibling})

        def forward():
            for step in range(1, 4):
                place = dst_of(row_of(chip - step, core))
                await_slot(place, base + step)
                remote(place, place, base + 4 + step, {"row": sibling})

        def wait():
            await_slot(dst_of(sibling), base)
            for step in range(1, 4):
                await_slot(dst_of(row_of(chip - step, 1 - core)), base + 4 + step)

        return forward, wait

    def spread_col_shared(src, dst_of):
        base = take("r", 8)
        for step in range(1, COLS):
            remote(src, dst_of(c, core), base + step, {"col": lax.rem(c + step, COLS)})

        def forward():
            for step in range(1, COLS):
                place = dst_of(lax.rem(c + COLS - step, COLS), core)
                await_slot(place, base + step)
                remote(place, place, base + 4 + step, {"row": sibling})

        def wait():
            for step in range(1, COLS):
                await_slot(dst_of(lax.rem(c + COLS - step, COLS), 1 - core), base + 4 + step)

        return forward, wait

    anc = [LAYERS - (LAYERS >> a) + g // 2 ** (a + 1) for a in range(TOPL)]
    my_rows = aligned(r, SLAB)
    my_k = aligned(c, KCH)
    my_cols = aligned(c, CG)
    half_src = aligned(core, SLAB)

    def half_rows(owner, half):
        return aligned(owner * 2 + half, SLAB)

    def lanes_of(owner):
        return pl.ds(pl.multiple_of(owner * CG, CG), CG)

    barrier = pltpu.get_barrier_semaphore()

    def greet(target):
        pl.semaphore_signal(barrier, inc=1, device_id=target, device_id_type=MESH)

    partners = []
    for a in range(TOPL - 1):
        span = 2**a
        partners.append(g + span - 2 * span * lax.rem(g // span, 2))
    quarter = g // 4
    source = jnp.where(quarter == 0, 15, jnp.where(quarter == 1, 8, jnp.where(quarter == 2, 7, 0)))
    edge = jnp.logical_or(jnp.logical_or(g == 0, g == 7), jnp.logical_or(g == 8, g == 15))
    first_target = jnp.where(g == 0, 12, jnp.where(g == 7, 8, jnp.where(g == 8, 4, 0)))
    for step in range(1, ROWS):
        greet({"row": lax.rem(r + step, ROWS)})
    for step in range(ROWS):
        greet({"row": lax.rem(r + step, ROWS), "gz": partners[0]})
    for step in range(1, COLS):
        greet({"col": lax.rem(c + step, COLS)})
    greet({"gz": partners[1]})
    greet({"gz": partners[2]})
    greet({"gz": source})

    c_x1 = local(rhs_local.at[pl.ds(0, NPL), :, my_cols], x1.at[:, my_rows, :])
    c_li1 = local(linv_local.at[pl.ds(0, NPL)], linv.at[pl.ds(0, NPL), my_k, :])
    c_ltree = local(l_tree, st_ltree)
    c_lpath = local(l_path, st_lpath)
    c_ltop = [local(l_top.at[anc[a]], st_ltop.at[a]) for a in range(3)]
    c_lit = [local(linv_top.at[anc[a]], linvt.at[a, my_k, :]) for a in range(TOPL)]
    c_uit = [local(uinv_top.at[anc[a]], uinvt.at[a, my_rows, :]) for a in range(TOPL)]
    c_rt = [local(rhs_top.at[anc[a], :, my_cols], st_rt.at[a]) for a in range(TOPL)]
    c_li2 = local(linv_local.at[pl.ds(NPL, NPL)], linv.at[pl.ds(NPL, NPL), my_k, :])
    c_rhs2 = local(rhs_local.at[pl.ds(NPL, NPL), :, my_cols], rhs2_own)
    c_utop = [local(u_top.at[anc[a]], st_utop.at[a]) for a in range(3)]
    c_utree = local(u_tree, st_utree)
    c_upath = local(u_path, st_upath)
    c_ui2 = local(uinv_local.at[pl.ds(NPL, NPL)], uinv2.at[:, my_rows, :])
    c_uiown = local(uinv_local, uinv_own)

    pl.semaphore_wait(barrier, ROWS - 1 + ROWS + COLS - 1 + 2 + jnp.where(edge, 4, 0))

    w_x1 = spread(
        "row", lambda peer: rhs_local.at[pl.ds(0, NPL), :, my_cols],
        lambda me: x1.at[:, aligned(me, SLAB), :],
    )
    f_li1, w_li1 = spread_col_shared(
        linv_local.at[pl.ds(0, NPL), half_src], lambda o, h: linv.at[pl.ds(0, NPL), half_rows(o, h), :]
    )
    odd = lax.rem(c, 2)

    def shifted(block):
        blank = jnp.zeros_like(block)
        low = jnp.concatenate([block, blank], axis=-1)
        high = jnp.concatenate([blank, block], axis=-1)
        return jnp.where(odd == 0, low, high)

    c_ltree.wait()
    for j in range(NPL):
        lt[c, j] = shifted(st_ltree[j])
    w_lt = spread("col", lambda peer: lt.at[c], lambda me: lt.at[me])
    f_li2, w_li2 = spread_col_shared(
        linv_local.at[pl.ds(NPL, NPL), half_src], lambda o, h: linv.at[pl.ds(NPL, NPL), half_rows(o, h), :]
    )
    c_lpath.wait()
    for m in range(TOPL):
        lp[c, pl.ds(m * SLAB, SLAB), :] = jnp.concatenate([st_lpath[k, m] for k in range(LOC)], axis=-1)
    w_lp = spread("col", lambda peer: lp.at[c], lambda me: lp.at[me])
    for copy in c_ltop:
        copy.wait()
    for b, (a, m) in enumerate(L_PAIRS):
        ltp1[c, b] = shifted(st_ltop[a, m])
    w_ltp1 = spread("col", lambda peer: ltp1.at[c], lambda me: ltp1.at[me])
    for copy in c_lit:
        copy.wait()
    f_lit, w_lit = spread_col_shared(
        linvt.at[:, half_rows(c, core), :], lambda o, h: linvt.at[:, half_rows(o, h), :]
    )
    for copy in c_uit:
        copy.wait()
    f_uit, w_uit = spread_row_shared(uinvt.at[:, my_rows, :], lambda me: uinvt.at[:, aligned(me, SLAB), :])

    eye = (
        lax.broadcasted_iota(jnp.int32, (CG, CG), 0) == lax.broadcasted_iota(jnp.int32, (CG, CG), 1)
    ).astype(F32).astype(BF16)
    for copy in c_rt:
        copy.wait()
    rt[...] = nt(eye, st_rt[...].reshape(TOPL * SLAB, CG)).astype(BF16)
    w_rr = spread("row", lambda peer: rt.at[aligned(peer, CP), :], lambda me: rr.at[me])
    rr[r] = rt[aligned(r, CP), :]
    c_ui2.wait()
    f_ui2, w_ui2 = spread_row_shared(uinv2.at[:, my_rows, :], lambda me: uinv2.at[:, aligned(me, SLAB), :])

    eye_k = eye[0:KCH, 0:KCH]

    def packed(stack):
        return nt(eye_k, stack).astype(BF16)

    for copy in c_utop:
        copy.wait()
    utp[0, my_k, :] = packed(jnp.concatenate([st_utop[2, 3], st_utop[0, 1], st_utop[0, 2], st_utop[0, 3]], axis=0))
    utp[1, my_k, :] = packed(st_utop[1].reshape(CG, KCH))
    c_utree.wait()
    utp[2, my_k, :] = packed(st_utree[...].reshape(CG, KCH))
    w_utp = spread("col", lambda peer: utp.at[:, my_k, :], lambda me: utp.at[:, aligned(me, KCH), :])
    c_upath.wait()
    for k in range(LOC):
        up[k, my_k, :] = packed(st_upath[k].reshape(CG, KCH))

    c_x1.wait()
    c_li1.wait()
    f_li1()
    w_x1()
    w_li1()
    for j in range(NPL):
        solved = mm(linv[j], x1[j])
        y[j] = solved
        ylow[j] = solved.astype(BF16)
    w_lt()
    terms = []
    for j in range(NPL):
        term = mm(lt[0, j] + lt[1, j], ylow[j, 0:CG, :]) + mm(lt[2, j] + lt[3, j], ylow[j, CG:W, :])
        terms.append(term)
    c_rhs2.wait()
    for i in range(NPL):
        value = rhs2_own[i].astype(F32)
        for j in range(NPL):
            value = value - jnp.where(parent[j] == i, 1.0, 0.0).astype(F32) * terms[j]
        s2f[i, my_rows, :] = value.astype(BF16)
    w_s2 = spread("row", lambda peer: s2f.at[:, my_rows, :], lambda me: s2f.at[:, aligned(me, SLAB), :])

    w_up = spread("col", lambda peer: up.at[:, my_k, :], lambda me: up.at[:, aligned(me, KCH), :])
    f_li2()
    w_lp()
    toward = jnp.zeros((TOPL * SLAB, CG), F32)
    for q in range(COLS):
        block = ylow[0:NPL, q * KCH:(q + 1) * KCH, :].reshape(NPL * KCH, CG)
        toward = toward + mm(lp[q, :, 0:NPL * KCH], block)

    c_li2.wait()
    w_li2()
    w_s2()
    for i in range(NPL):
        solved = mm(linv[NPL + i], s2f[i])
        y[NPL + i] = solved
        ylow[NPL + i] = solved.astype(BF16)
    for q in range(COLS):
        block = ylow[NPL:LOC, q * KCH:(q + 1) * KCH, :].reshape(NPL * KCH, CG)
        toward = toward + mm(lp[q, :, NPL * KCH:LOC * KCH], block)
    tt[...] = nt(eye, toward.astype(BF16)).astype(BF16)
    base = take("r", 2 * ROWS)
    remote(tt.at[aligned(r, CP), :], rv.at[1, r], base + ROWS, {"gz": partners[0]})
    for step in range(1, ROWS):
        peer = lax.rem(r + step, ROWS)
        remote(tt.at[aligned(peer, CP), :], rv.at[1, r], base + ROWS + step, {"row": peer, "gz": partners[0]})
        remote(tt.at[aligned(peer, CP), :], rv.at[0, r], base + step, {"row": peer})
    rv[0, r] = tt[aligned(r, CP), :]

    def w_rv():
        await_slot(rv.at[1, r], base + ROWS)
        for step in range(1, ROWS):
            sender = lax.rem(r + ROWS - step, ROWS)
            await_slot(rv.at[0, sender], base + step)
            await_slot(rv.at[1, sender], base + ROWS + step)

    w_ltp1()
    for b in range(len(L_PAIRS)):
        ltp[b, my_rows, :] = jnp.concatenate([ltp1[0, b] + ltp1[1, b], ltp1[2, b] + ltp1[3, b]], axis=-1)
    f_ltp, w_ltp = spread_row_shared(ltp.at[:, my_rows, :], lambda me: ltp.at[:, aligned(me, SLAB), :])
    f_lit()

    slot_of_lane = lax.broadcasted_iota(jnp.int32, (CP, CG), 1) // SLAB

    def by_level(tiles, m):
        halves = []
        for q in range(2):
            total = None
            for s in range(4):
                piece = tiles[4 * q + s]
                if s != m:
                    piece = pltpu.roll(piece, (s - m) * SLAB % CG, 1)
                total = piece if total is None else jnp.where(slot_of_lane == s, piece, total)
            halves.append(total)
        return jnp.concatenate(halves, axis=-1)

    w_rr()
    rr_tiles = [rr[q].astype(F32) for q in range(ROWS)]
    top_rhs = [by_level(rr_tiles, m) for m in range(TOPL)]
    w_utp()
    f_ut, w_ut = spread_row_shared(utp, lambda me: ut.at[:, :, lanes_of(me)])
    c_ut = local(utp, ut.at[:, :, lanes_of(r)])
    w_rv()
    rv_tiles = [rv[0, q].astype(F32) + rv[1, q].astype(F32) for q in range(ROWS)]
    pend = [by_level(rv_tiles, m) for m in range(TOPL)]
    f_ltp()
    w_lit()
    w_ltp()

    top_y = []
    for a in range(TOPL):
        count = TOPL - a
        base = Z_BASE[a]
        if a > 0:
            place = pl.ds(base, count)
            for m in range(a, TOPL):
                zs[base + m - a] = pend[m].astype(BF16)
            slot = take("r")
            if a < TOPL - 1:
                remote(zs.at[place], zr.at[place], slot, {"gz": partners[a]})
            else:
                last_sends = [
                    pltpu.make_async_remote_copy(
                        src_ref=zs.at[place], dst_ref=zr.at[place], send_sem=ssem.at[take("s")],
                        recv_sem=rsem.at[slot], device_id={"gz": first_target + step}, device_id_type=MESH,
                    )
                    for step in range(4)
                ]

                @pl.when(edge)
                def _():
                    for copy in last_sends:
                        copy.start()

            if a == 1:
                f_uit()
                f_ui2()
                w_up()
                w_us = spread(
                    "row", lambda peer: up.at[:, aligned(peer, SLAB), :], lambda me: us.at[:, :, lanes_of(me)]
                )
                c_us = local(up.at[:, my_rows, :], us.at[:, :, lanes_of(r)])
            if a == 3:
                f_ut()
            await_slot(zr.at[place], slot)
            for m in range(a, TOPL):
                pend[m] = pend[m] + zr[base + m - a].astype(F32)
        solved = nt((top_rhs[a] - pend[a]).astype(BF16), linvt[a])
        top_y.append(solved)
        low = solved.astype(BF16)
        for b, (below, m) in enumerate(L_PAIRS):
            if below == a:
                pend[m] = pend[m] + nt(low, ltp[b])

    w_uit()
    c_ut.wait()
    w_ut()
    tiles = [jnp.zeros((CP, CG), F32) for _ in range(ROWS)]
    for a in reversed(range(TOPL)):
        value = top_y[a]
        if a < TOPL - 1:
            if a == 2:
                known = [pltpu.roll(tile, SLAB, 1) for tile in tiles]
            else:
                known = tiles
            above = jnp.concatenate(known, axis=-1).astype(BF16)
            value = value - nt(above, ut[0 if a != 1 else 1])
        solved = nt(value.astype(BF16), uinvt[a])
        for q in range(2):
            half = solved[:, q * CG:(q + 1) * CG]
            for s in range(4):
                piece = half if a == s else pltpu.roll(half, (a - s) * SLAB % CG, 1)
                tiles[4 * q + s] = jnp.where(slot_of_lane == a, piece, tiles[4 * q + s])
    my_cp = aligned(r, CP)
    xp[my_cp, :] = jnp.concatenate(tiles, axis=-1).astype(BF16)
    w_xp = spread("row", lambda peer: xp.at[my_cp, :], lambda me: xp.at[aligned(me, CP), :])

    lane_slot = lax.rem(lax.broadcasted_iota(jnp.int32, (W, ROWS * CG), 1) // SLAB, NPL)
    for j in range(NPL):
        tree_w[j] = jnp.where(lane_slot == j, ut[2], jnp.zeros((W, ROWS * CG), BF16))
    c_us.wait()
    w_us()
    w_xp()
    path = xp[...]
    path_term2 = nt(us[NPL:LOC].reshape(NPL * SLAB, ROWS * CG), path)
    for i in range(NPL):
        value = y[NPL + i, my_rows, :] - path_term2[i * SLAB:(i + 1) * SLAB, :]
        sb2[i, my_rows, :] = value.astype(BF16)
    w_sb2 = spread("row", lambda peer: sb2.at[:, my_rows, :], lambda me: sb2.at[:, aligned(me, SLAB), :])
    path_term1 = nt(us[0:NPL].reshape(NPL * SLAB, ROWS * CG), path)
    for j in range(NPL):
        value = y[j, my_rows, :] - path_term1[j * SLAB:(j + 1) * SLAB, :]
        sb1[j, my_rows, :] = value.astype(BF16)
    w_sb1 = spread("row", lambda peer: sb1.at[:, my_rows, :], lambda me: sb1.at[:, aligned(me, SLAB), :])
    own_path = nt(eye, xp[:, lanes_of(r)])
    for m in range(TOPL):
        out_p[m] = own_path[m * SLAB:(m + 1) * SLAB, :]
    piece_rows = SLAB // COLS

    def out_rows(peer):
        return pl.ds(pl.multiple_of(peer * piece_rows, piece_rows), piece_rows)

    w_outp = spread(
        "col", lambda peer: out_p.at[:, out_rows(peer), :], lambda me: x_path.at[0, :, :, lanes_of(me)]
    )
    c_outp = local(out_p.at[:, out_rows(c), :], x_path.at[0, :, :, my_cols])

    w_ui2()
    c_uiown.wait()
    w_sb2()
    for i in range(NPL):
        x2low[i] = mm(uinv2[i], sb2[i]).astype(BF16)
    parent_x = [x2low[parent[j]].reshape(ROWS, 1, SLAB, CG) for j in range(NPL)]
    stacked = jnp.concatenate(parent_x, axis=1).reshape(ROWS * NPL * SLAB, CG)
    trees = [mm(tree_w[j], stacked) for j in range(NPL)]
    for i in range(NPL):
        out_l[NPL + i] = mm(uinv_own[NPL + i], sb2[i])

    def send_out(first):
        part = pl.ds(first, NPL)
        wait = spread(
            "col", lambda peer: out_l.at[part, out_rows(peer), :], lambda me: x_local.at[part, :, lanes_of(me)]
        )
        return wait, local(out_l.at[part, out_rows(c), :], x_local.at[part, :, my_cols])

    w_out2, c_out2 = send_out(NPL)
    w_sb1()
    for j in range(NPL):
        out_l[j] = mm(uinv_own[j], (sb1[j].astype(F32) - trees[j]).astype(BF16))
    w_out1, c_out1 = send_out(0)
    w_outp()
    w_out2()
    w_out1()
    for copy in (c_outp, c_out2, c_out1):
        copy.wait()
    for copy in pending_sends:
        copy.wait_send()

    @pl.when(edge)
    def _():
        for copy in last_sends:
            copy.wait_send()


def per_device(*arrays):
    arrays = list(arrays)
    for index in (4, 5, 6):
        arrays[index] = jnp.swapaxes(arrays[index], -1, -2)
    any_space = pl.BlockSpec(memory_space=pl.ANY)
    vmem = pltpu.VMEM
    scratch = [
        vmem((NPL, SLAB, KCH), BF16),
        vmem((LOC, TOPL, SLAB, KCH), BF16),
        vmem((3, TOPL, SLAB, KCH), BF16),
        vmem((NPL, SLAB, KCH), BF16),
        vmem((LOC, TOPL, SLAB, KCH), BF16),
        vmem((3, TOPL, SLAB, KCH), BF16),
        vmem((LOC, SLAB, W), BF16),
        vmem((NPL, SLAB, CG), BF16),
        vmem((TOPL, SLAB, CG), BF16),
        vmem((NPL, W, CG), BF16),
        vmem((LOC, W, W), BF16),
        vmem((COLS, NPL, SLAB, CG), BF16),
        vmem((COLS, TOPL * SLAB, LOC * KCH), BF16),
        vmem((COLS, 6, SLAB, CG), BF16),
        vmem((6, W, W), BF16),
        vmem((TOPL, W, W), BF16),
        vmem((TOPL, W, W), BF16),
        vmem((NPL, W, W), BF16),
        vmem((LOC, W, CG), BF16),
        vmem((LOC, SLAB, ROWS * CG), BF16),
        vmem((3, W, CG), BF16),
        vmem((3, W, ROWS * CG), BF16),
        vmem((NPL, W, ROWS * CG), BF16),
        vmem((LOC, W, CG), F32),
        vmem((LOC, W, CG), BF16),
        vmem((NPL, W, CG), BF16),
        vmem((CG, TOPL * SLAB), BF16),
        vmem((2, ROWS, CP, CG), BF16),
        vmem((CG, TOPL * SLAB), BF16),
        vmem((ROWS, CP, CG), BF16),
        vmem((10, CP, W), BF16),
        vmem((10, CP, W), BF16),
        vmem((CG, ROWS * CG), BF16),
        vmem((NPL, W, CG), BF16),
        vmem((NPL, W, CG), BF16),
        vmem((NPL, W, CG), BF16),
        vmem((LOC, SLAB, CG), F32),
        vmem((TOPL, SLAB, CG), F32),
        pltpu.SemaphoreType.DMA((48,)),
        pltpu.SemaphoreType.DMA((200,)),
        pltpu.SemaphoreType.DMA((200,)),
    ]
    return pl.pallas_call(
        kernel,
        out_shape=(
            jax.ShapeDtypeStruct((LOC, SLAB // COLS, R), F32),
            jax.ShapeDtypeStruct((1, TOPL, SLAB // COLS, R), F32),
        ),
        in_specs=[pl.BlockSpec(memory_space=pltpu.SMEM)] + [any_space] * 12,
        out_specs=(any_space, any_space),
        scratch_shapes=scratch,
        compiler_params=pltpu.CompilerParams(
            collective_id=0, has_side_effects=True, vmem_limit_bytes=60 * 1024 * 1024
        ),
    )(*arrays)


def solution(mesh):
    placed = (
        P("gz"),
        P("gz", "row", "col"),
        P("gz", None, "row", "col"),
        P(None, None, "row", "col"),
        P("gz", "col", "row"),
        P("gz", None, "col", "row"),
        P(None, None, "col", "row"),
        P("gz", "col", None),
        P(None, "col", None),
        P("gz", "row", None),
        P(None, "row", None),
        P("gz", "row", None),
        P(None, "row", None),
    )
    return jax.shard_map(
        per_device,
        mesh=mesh,
        in_specs=placed,
        out_specs=(P("gz", ("row", "col"), None), P("gz", None, ("row", "col"), None)),
        check_vma=False,
    )
```

```python
import functools

import jax
import jax.numpy as jnp
from jax import lax
from jax.experimental import pallas as pl
from jax.experimental.pallas import tpu as pltpu
from jax.sharding import PartitionSpec as P

F32 = jnp.float32
BF16 = jnp.bfloat16
MESH = pl.DeviceIdType.MESH
ROWS, COLS, LAYERS = 8, 4, 16
NPL, LOC, TOPL = 4, 8, 4
W, R = 256, 512
SLAB, KCH = W // ROWS, W // COLS
CG = R // COLS
CP = CG // ROWS
L_PAIRS = ((0, 1), (0, 2), (0, 3), (1, 2), (1, 3), (2, 3), (3, 3), (3, 3))
QUAD = 4


def nt(a, b):
    return lax.dot_general(a, b, (((1,), (1,)), ((), ())), preferred_element_type=F32)


def mm(a, b):
    return jnp.dot(a, b, preferred_element_type=F32)


def aligned(value, size):
    return pl.ds(pl.multiple_of(value * size, size), size)


def kernel(
    parent, l_tree, l_path, l_top, u_tree, u_path, u_top, linv_local, linv_top, uinv_local,
    uinv_top, rhs_local, rhs_top, x_local, x_path,
    st_ltree, st_lpath, st_ltop, st_utree, st_upath, st_utop, uinv_own, rhs2_own, st_rt,
    x1, linv, lt, lp, ltp1, ltp, linvt, uinvt, uinv2, up, us, utp, ut, tree_w, mprod, vprod, nprod,
    y, ylow, s2f, tt, rv, rt, rr, zs1, zr1, zs2, zr2, xp, sb2, x2low, sb1, out_l, out_p,
    lsem, ssem, rsem,
):
    r = lax.axis_index("row")
    c = lax.axis_index("col")
    g = lax.axis_index("gz")
    chip, core = r // 2, lax.rem(r, 2)
    sibling = chip * 2 + 1 - core
    counters = {"l": 0, "s": 0, "r": 0}
    pending_sends = []

    def take(kind, count=1):
        first = counters[kind]
        counters[kind] += count
        return first

    def local(src, dst):
        copy = pltpu.make_async_copy(src, dst, lsem.at[take("l")])
        copy.start()
        return copy

    def remote(src, dst, slot, target):
        copy = pltpu.make_async_remote_copy(
            src_ref=src, dst_ref=dst, send_sem=ssem.at[take("s")], recv_sem=rsem.at[slot],
            device_id=target, device_id_type=MESH,
        )
        copy.start()
        pending_sends.append(copy)

    def await_slot(dst, slot):
        pltpu.make_async_remote_copy(
            src_ref=dst, dst_ref=dst, send_sem=ssem.at[0], recv_sem=rsem.at[slot],
            device_id={"row": r}, device_id_type=MESH,
        ).wait_recv()

    def spread(axis, src_of, dst_of):
        me, size = (r, ROWS) if axis == "row" else (c, COLS)
        base = take("r", size)
        for step in range(1, size):
            peer = lax.rem(me + step, size)
            remote(src_of(peer), dst_of(me), base + step, {axis: peer})

        def wait():
            for step in range(1, size):
                await_slot(dst_of(lax.rem(me + size - step, size)), base + step)

        return wait

    def row_of(other_chip, other_core):
        return lax.rem(other_chip + 4, 4) * 2 + other_core

    def spread_row_shared(src, dst_of):
        base = take("r", 8)
        for step in range(1, 4):
            remote(src, dst_of(r), base + step, {"row": row_of(chip + step, core)})
        remote(src, dst_of(r), base, {"row": sibling})

        def forward():
            for step in range(1, 4):
                place = dst_of(row_of(chip - step, core))
                await_slot(place, base + step)
                remote(place, place, base + 4 + step, {"row": sibling})

        def wait():
            await_slot(dst_of(sibling), base)
            for step in range(1, 4):
                await_slot(dst_of(row_of(chip - step, 1 - core)), base + 4 + step)

        return forward, wait

    def spread_col_shared(src, dst_of):
        base = take("r", 8)
        for step in range(1, COLS):
            remote(src, dst_of(c, core), base + step, {"col": lax.rem(c + step, COLS)})

        def forward():
            for step in range(1, COLS):
                place = dst_of(lax.rem(c + COLS - step, COLS), core)
                await_slot(place, base + step)
                remote(place, place, base + 4 + step, {"row": sibling})

        def wait():
            for step in range(1, COLS):
                await_slot(dst_of(lax.rem(c + COLS - step, COLS), 1 - core), base + 4 + step)

        return forward, wait

    anc = [LAYERS - (LAYERS >> a) + g // 2 ** (a + 1) for a in range(TOPL)]
    other = LAYERS - (LAYERS >> 2) + 1 - g // (LAYERS // 2)
    my_rows = aligned(r, SLAB)
    my_k = aligned(c, KCH)
    my_cols = aligned(c, CG)
    half_src = aligned(core, SLAB)

    def half_rows(owner, half):
        return aligned(owner * 2 + half, SLAB)

    def lanes_of(owner):
        return pl.ds(pl.multiple_of(owner * CG, CG), CG)

    c_ltree = local(l_tree, st_ltree)
    c_lpath = local(l_path, st_lpath)
    c_ltop = [local(l_top.at[node], st_ltop.at[n]) for n, node in enumerate(anc[0:3] + [other])]

    barrier = pltpu.get_barrier_semaphore()

    def greet(target):
        pl.semaphore_signal(barrier, inc=1, device_id=target, device_id_type=MESH)

    near = g + 1 - 2 * lax.rem(g, 2)
    across = g + 2 - 4 * lax.rem(g // 2, 2)
    quad, place_in_quad = g // QUAD, lax.rem(g, QUAD)
    quads = LAYERS // QUAD
    upper = place_in_quad // (QUAD - 1)
    speaks = jnp.logical_or(place_in_quad == 0, place_in_quad == QUAD - 1)
    half = place_in_quad // 2

    def quad_at(offset):
        return lax.rem(quad + quads + offset, quads) * QUAD

    sources = [quad_at(1), quad_at(-1) + QUAD - 1, quad_at(2) + (QUAD - 1) * (1 - half)]
    direction = 2 * upper - 1
    targets = [(quad_at(2) + 2 * (1 - upper) + step, 2) for step in range(2)]
    targets += [(quad_at(direction) + step, upper) for step in range(QUAD)]
    for source in sources:
        greet({"gz": source})
    greet({"gz": across})
    for step in range(ROWS):
        greet({"row": lax.rem(r + step, ROWS), "gz": near})
    for step in range(1, ROWS):
        greet({"row": lax.rem(r + step, ROWS)})
    for step in range(1, COLS):
        greet({"col": lax.rem(c + step, COLS)})

    pl.semaphore_wait(barrier, ROWS - 1 + ROWS + COLS - 1 + 1 + jnp.where(speaks, 6, 0))

    w_x1 = spread(
        "row", lambda peer: rhs_local.at[pl.ds(0, NPL), :, my_cols],
        lambda me: x1.at[:, aligned(me, SLAB), :],
    )
    f_li1, w_li1 = spread_col_shared(
        linv_local.at[pl.ds(0, NPL), half_src], lambda o, h: linv.at[pl.ds(0, NPL), half_rows(o, h), :]
    )
    c_x1 = local(rhs_local.at[pl.ds(0, NPL), :, my_cols], x1.at[:, my_rows, :])
    c_li1 = local(linv_local.at[pl.ds(0, NPL)], linv.at[pl.ds(0, NPL), my_k, :])
    c_lit = [local(linv_top.at[node], linvt.at[n, my_k, :]) for n, node in enumerate(anc + [other])]
    c_uit = [local(uinv_top.at[anc[a]], uinvt.at[a, my_rows, :]) for a in range(TOPL)]
    c_rt = [local(rhs_top.at[node, :, my_cols], st_rt.at[n]) for n, node in enumerate(anc + [other])]
    c_li2 = local(linv_local.at[pl.ds(NPL, NPL)], linv.at[pl.ds(NPL, NPL), my_k, :])
    c_rhs2 = local(rhs_local.at[pl.ds(NPL, NPL), :, my_cols], rhs2_own)
    c_utop = [local(u_top.at[anc[a]], st_utop.at[a]) for a in range(3)]
    c_utree = local(u_tree, st_utree)
    c_upath = local(u_path, st_upath)
    c_ui2 = local(uinv_local.at[pl.ds(NPL, NPL)], uinv2.at[:, my_rows, :])
    c_uiown = local(uinv_local, uinv_own)

    c_ltree.wait()
    for b in range(NPL // 2):
        lt[c, b] = jnp.concatenate([st_ltree[2 * b], st_ltree[2 * b + 1]], axis=-1)
    w_lt = spread("col", lambda peer: lt.at[c], lambda me: lt.at[me])
    for copy in c_ltop:
        copy.wait()
    for b in range(len(L_PAIRS) // 2):
        (a1, m1), (a2, m2) = L_PAIRS[2 * b], L_PAIRS[2 * b + 1]
        ltp1[c, b] = jnp.concatenate([st_ltop[a1, m1], st_ltop[a2, m2]], axis=-1)
    w_ltp1 = spread("col", lambda peer: ltp1.at[c], lambda me: ltp1.at[me])
    f_li2, w_li2 = spread_col_shared(
        linv_local.at[pl.ds(NPL, NPL), half_src], lambda o, h: linv.at[pl.ds(NPL, NPL), half_rows(o, h), :]
    )
    c_lpath.wait()
    for m in range(TOPL):
        lp[c, pl.ds(m * SLAB, SLAB), :] = jnp.concatenate([st_lpath[k, m] for k in range(LOC)], axis=-1)
    w_lp = spread("col", lambda peer: lp.at[c], lambda me: lp.at[me])

    def unpaired(pieces, b):
        half = pl.ds(b % 2 * KCH, KCH)
        return jnp.concatenate([pieces[q, b // 2, :, half] for q in range(COLS)], axis=-1)

    for copy in c_lit:
        copy.wait()
    f_lit, w_lit = spread_col_shared(
        linvt.at[:, half_rows(c, core), :], lambda o, h: linvt.at[:, half_rows(o, h), :]
    )
    for copy in c_uit:
        copy.wait()
    f_uit, w_uit = spread_row_shared(uinvt.at[:, my_rows, :], lambda me: uinvt.at[:, aligned(me, SLAB), :])

    c_ui2.wait()
    f_ui2, w_ui2 = spread_row_shared(uinv2.at[:, my_rows, :], lambda me: uinv2.at[:, aligned(me, SLAB), :])

    c_x1.wait()
    c_li1.wait()
    f_li1()
    w_x1()
    w_li1()
    for j in range(NPL):
        solved = mm(linv[j], x1[j])
        y[j] = solved
        ylow[j] = solved.astype(BF16)
    w_lt()
    terms = []
    for j in range(NPL):
        terms.append(mm(unpaired(lt, j), ylow[j]))
    c_rhs2.wait()
    for i in range(NPL):
        value = rhs2_own[i].astype(F32)
        for j in range(NPL):
            value = value - jnp.where(parent[j] == i, 1.0, 0.0).astype(F32) * terms[j]
        s2f[i, my_rows, :] = value.astype(BF16)
    w_s2 = spread("row", lambda peer: s2f.at[:, my_rows, :], lambda me: s2f.at[:, aligned(me, SLAB), :])

    eye = (
        lax.broadcasted_iota(jnp.int32, (CG, CG), 0) == lax.broadcasted_iota(jnp.int32, (CG, CG), 1)
    ).astype(F32).astype(BF16)
    for copy in c_rt:
        copy.wait()
    rt[:, 0:CG] = nt(eye, st_rt[0:TOPL].reshape(TOPL * SLAB, CG)).astype(BF16)
    rt[:, CG:2 * CG] = nt(eye, jnp.concatenate([st_rt[TOPL]] * 4, axis=0)).astype(BF16)
    w_rr = spread("row", lambda peer: rt.at[aligned(peer, CP), :], lambda me: rr.at[me])
    rr[r] = rt[aligned(r, CP), :]
    w_ltp1()
    for b in range(len(L_PAIRS) - 1):
        ltp[b, my_rows, :] = unpaired(ltp1, b)
    f_ltp, w_ltp = spread_row_shared(ltp.at[:, my_rows, :], lambda me: ltp.at[:, aligned(me, SLAB), :])
    f_li2()

    eye_k = eye[0:KCH, 0:KCH]

    def packed(stack):
        return nt(eye_k, stack).astype(BF16)

    for copy in c_utop:
        copy.wait()
    utp[0, my_k, :] = packed(jnp.concatenate([st_utop[2, 3], st_utop[0, 1], st_utop[0, 2], st_utop[0, 3]], axis=0))
    utp[1, my_k, :] = packed(st_utop[1].reshape(CG, KCH))
    c_utree.wait()
    utp[2, my_k, :] = packed(st_utree[...].reshape(CG, KCH))
    w_utp = spread("col", lambda peer: utp.at[:, my_k, :], lambda me: utp.at[:, aligned(me, KCH), :])
    c_upath.wait()
    for k in range(LOC):
        up[k, my_k, :] = packed(st_upath[k].reshape(CG, KCH))

    w_up = spread("col", lambda peer: up.at[:, my_k, :], lambda me: up.at[:, aligned(me, KCH), :])
    w_lp()
    toward = jnp.zeros((TOPL * SLAB, CG), F32)
    for q in range(COLS):
        block = ylow[0:NPL, q * KCH:(q + 1) * KCH, :].reshape(NPL * KCH, CG)
        toward = toward + mm(lp[q, :, 0:NPL * KCH], block)

    c_li2.wait()
    w_li2()
    w_s2()
    for i in range(NPL):
        solved = mm(linv[NPL + i], s2f[i])
        y[NPL + i] = solved
        ylow[NPL + i] = solved.astype(BF16)
    for q in range(COLS):
        block = ylow[NPL:LOC, q * KCH:(q + 1) * KCH, :].reshape(NPL * KCH, CG)
        toward = toward + mm(lp[q, :, NPL * KCH:LOC * KCH], block)
    tt[...] = nt(eye, toward.astype(BF16)).astype(BF16)
    base = take("r", 2 * ROWS)
    remote(tt.at[aligned(r, CP), :], rv.at[1, r], base + ROWS, {"gz": near})
    for step in range(1, ROWS):
        peer = lax.rem(r + step, ROWS)
        remote(tt.at[aligned(peer, CP), :], rv.at[1, r], base + ROWS + step, {"row": peer, "gz": near})
        remote(tt.at[aligned(peer, CP), :], rv.at[0, r], base + step, {"row": peer})
    rv[0, r] = tt[aligned(r, CP), :]

    def w_rv():
        await_slot(rv.at[1, r], base + ROWS)
        for step in range(1, ROWS):
            sender = lax.rem(r + ROWS - step, ROWS)
            await_slot(rv.at[0, sender], base + step)
            await_slot(rv.at[1, sender], base + ROWS + step)

    f_lit()

    slot_of_lane = lax.shift_right_logical(lax.broadcasted_iota(jnp.int32, (CP, CG), 1), 5)

    def by_level(tiles, m):
        halves = []
        for q in range(2):
            total = None
            for s in range(4):
                piece = tiles[4 * q + s]
                if s != m:
                    piece = pltpu.roll(piece, (s - m) * SLAB % CG, 1)
                total = piece if total is None else jnp.where(slot_of_lane == s, piece, total)
            halves.append(total)
        return jnp.concatenate(halves, axis=-1)

    w_rr()
    rr_tiles = [rr[q, :, 0:CG].astype(F32) for q in range(ROWS)]
    top_rhs = [by_level(rr_tiles, m) for m in range(TOPL)]
    top_rhs.append(by_level([rr[q, :, CG:2 * CG].astype(F32) for q in range(ROWS)], 0))
    f_ltp()
    w_rv()
    rv_tiles = [rv[0, q].astype(F32) + rv[1, q].astype(F32) for q in range(ROWS)]
    pend = [by_level(rv_tiles, m) for m in range(TOPL)]
    w_lit()
    w_ltp()

    def solve_zero():
        solved = nt((top_rhs[0] - pend[0]).astype(BF16), linvt[0])
        low = solved.astype(BF16)
        for m in range(1, TOPL):
            pend[m] = pend[m] + nt(low, ltp[m - 1])
        return low

    y_low = [solve_zero()]
    for m in range(1, TOPL):
        zs1[m - 1] = pend[m].astype(BF16)
    slot = take("r")
    remote(zs1, zr1, slot, {"gz": across})
    w_utp()
    f_ut, w_ut = spread_row_shared(utp, lambda me: ut.at[:, :, lanes_of(me)])
    c_ut = local(utp, ut.at[:, :, lanes_of(r)])
    f_uit()
    f_ui2()
    for n, (b, node) in enumerate(((3, 1), (4, 1), (5, 2), (6, 4))):
        mprod[n] = mm(ltp[b], linvt[node]).astype(BF16)
    await_slot(zr1, slot)
    for m in range(1, TOPL):
        pend[m] = pend[m] + zr1[m - 1].astype(F32)

    low = (top_rhs[1] - pend[1]).astype(BF16)
    for m in range(2, TOPL):
        pend[m] = pend[m] + nt(low, mprod[m - 2])
        zs2[m - 2] = pend[m].astype(BF16)
    slot = take("r", 3)
    speeches = [
        pltpu.make_async_remote_copy(
            src_ref=zs2, dst_ref=zr2.at[where], send_sem=ssem.at[take("s")],
            recv_sem=rsem.at[slot + where], device_id={"gz": target}, device_id_type=MESH,
        )
        for target, where in targets
    ]

    @pl.when(speaks)
    def _():
        for copy in speeches:
            copy.start()

    y_low.append(nt(low, linvt[1]).astype(BF16))
    w_up()
    w_us = spread("row", lambda peer: up.at[:, aligned(peer, SLAB), :], lambda me: us.at[:, :, lanes_of(me)])
    c_us = local(up.at[:, my_rows, :], us.at[:, :, lanes_of(r)])
    w_uit()
    vprod[...] = mm(uinvt[TOPL - 1], linvt[TOPL - 1]).astype(BF16)
    known_x = [nt(y_low[n], uinvt[n]) for n in range(2)]
    f_ut()
    c_ut.wait()
    w_ut()
    for n, tile in enumerate((0, 1, 0)):
        nprod[n] = mm(uinvt[n], ut[tile]).astype(BF16)
    for where in range(3):
        await_slot(zr2.at[where], slot + where)
    even = lax.rem(quad, 2) == 0
    after, before, opposite = (zr2[where, 0].astype(F32) for where in range(3))
    own_sum = pend[2] + jnp.where(even, after, before)
    other_sum = opposite + jnp.where(even, before, after)
    root_sum = pend[3] + zr2[0, 1].astype(F32) + zr2[1, 1].astype(F32) + zr2[2, 1].astype(F32)
    low = (top_rhs[2] - own_sum).astype(BF16)
    root_sum = root_sum + nt(low, mprod[2]) + nt((top_rhs[4] - other_sum).astype(BF16), mprod[3])
    known_x.append(nt(nt(low, linvt[2]).astype(BF16), uinvt[2]))
    known_x.append(nt((top_rhs[3] - root_sum).astype(BF16), vprod[...]))

    tiles = [jnp.zeros((CP, CG), F32) for _ in range(ROWS)]
    for a in reversed(range(TOPL)):
        solved = known_x[a]
        if a < TOPL - 1:
            if a == 2:
                known = [pltpu.roll(tile, SLAB, 1) for tile in tiles]
            else:
                known = tiles
            above = jnp.concatenate(known, axis=-1).astype(BF16)
            solved = solved - nt(above, nprod[a])
        for q in range(2):
            half = solved[:, q * CG:(q + 1) * CG]
            for s in range(4):
                piece = half if a == s else pltpu.roll(half, (a - s) * SLAB % CG, 1)
                tiles[4 * q + s] = jnp.where(slot_of_lane == a, piece, tiles[4 * q + s])
    my_cp = aligned(r, CP)
    xp[my_cp, :] = jnp.concatenate(tiles, axis=-1).astype(BF16)
    w_xp = spread("row", lambda peer: xp.at[my_cp, :], lambda me: xp.at[aligned(me, CP), :])

    lane_slot = lax.shift_right_logical(lax.broadcasted_iota(jnp.int32, (8, CG), 1), 5)
    for j in range(NPL):
        mask = jnp.where(lane_slot == j, 1.0, 0.0).astype(F32)[0:1, :].astype(BF16)
        for q in range(ROWS):
            tree_w[j, :, q * CG:(q + 1) * CG] = ut[2, :, q * CG:(q + 1) * CG] * mask
    c_us.wait()
    w_us()
    w_xp()
    path = xp[...]
    path_term2 = nt(us[NPL:LOC].reshape(NPL * SLAB, ROWS * CG), path)
    for i in range(NPL):
        value = y[NPL + i, my_rows, :] - path_term2[i * SLAB:(i + 1) * SLAB, :]
        sb2[i, my_rows, :] = value.astype(BF16)
    f_sb2, w_sb2 = spread_row_shared(sb2.at[:, my_rows, :], lambda me: sb2.at[:, aligned(me, SLAB), :])
    path_term1 = nt(us[0:NPL].reshape(NPL * SLAB, ROWS * CG), path)
    for j in range(NPL):
        value = y[j, my_rows, :] - path_term1[j * SLAB:(j + 1) * SLAB, :]
        sb1[j, my_rows, :] = value.astype(BF16)
    f_sb1, w_sb1 = spread_row_shared(sb1.at[:, my_rows, :], lambda me: sb1.at[:, aligned(me, SLAB), :])
    own_path = nt(eye, xp[:, lanes_of(r)])
    for m in range(TOPL):
        out_p[m] = own_path[m * SLAB:(m + 1) * SLAB, :]
    piece_rows = SLAB // COLS

    def out_rows(peer):
        return pl.ds(pl.multiple_of(peer * piece_rows, piece_rows), piece_rows)

    w_outp = spread(
        "col", lambda peer: out_p.at[:, out_rows(peer), :], lambda me: x_path.at[0, :, :, lanes_of(me)]
    )
    c_outp = local(out_p.at[:, out_rows(c), :], x_path.at[0, :, :, my_cols])

    w_ui2()
    c_uiown.wait()
    f_sb2()
    f_sb1()
    w_sb2()
    for i in range(NPL):
        x2low[i] = mm(uinv2[i], sb2[i]).astype(BF16)
    parent_x = [x2low[parent[j]].reshape(ROWS, 1, SLAB, CG) for j in range(NPL)]
    stacked = jnp.concatenate(parent_x, axis=1).reshape(ROWS * NPL * SLAB, CG)
    trees = [mm(tree_w[j], stacked) for j in range(NPL)]
    for i in range(NPL):
        out_l[NPL + i] = mm(uinv_own[NPL + i], sb2[i])

    def send_out(first):
        part = pl.ds(first, NPL)
        wait = spread(
            "col", lambda peer: out_l.at[part, out_rows(peer), :], lambda me: x_local.at[part, :, lanes_of(me)]
        )
        return wait, local(out_l.at[part, out_rows(c), :], x_local.at[part, :, my_cols])

    w_out2, c_out2 = send_out(NPL)
    w_sb1()
    for j in range(NPL):
        out_l[j] = mm(uinv_own[j], (sb1[j].astype(F32) - trees[j]).astype(BF16))
    w_out1, c_out1 = send_out(0)
    w_outp()
    w_out2()
    w_out1()
    for copy in (c_outp, c_out2, c_out1):
        copy.wait()
    for copy in pending_sends:
        copy.wait_send()

    @pl.when(speaks)
    def _():
        for copy in speeches:
            copy.wait_send()


def per_device(*arrays):
    arrays = list(arrays)
    for index in (4, 5, 6):
        arrays[index] = jnp.swapaxes(arrays[index], -1, -2)
    any_space = pl.BlockSpec(memory_space=pl.ANY)
    vmem = pltpu.VMEM
    scratch = [
        vmem((NPL, SLAB, KCH), BF16),
        vmem((LOC, TOPL, SLAB, KCH), BF16),
        vmem((4, TOPL, SLAB, KCH), BF16),
        vmem((NPL, SLAB, KCH), BF16),
        vmem((LOC, TOPL, SLAB, KCH), BF16),
        vmem((3, TOPL, SLAB, KCH), BF16),
        vmem((LOC, SLAB, W), BF16),
        vmem((NPL, SLAB, CG), BF16),
        vmem((TOPL + 1, SLAB, CG), BF16),
        vmem((NPL, W, CG), BF16),
        vmem((LOC, W, W), BF16),
        vmem((COLS, NPL // 2, SLAB, CG), BF16),
        vmem((COLS, TOPL * SLAB, LOC * KCH), BF16),
        vmem((COLS, 4, SLAB, CG), BF16),
        vmem((7, W, W), BF16),
        vmem((TOPL + 1, W, W), BF16),
        vmem((TOPL, W, W), BF16),
        vmem((NPL, W, W), BF16),
        vmem((LOC, W, CG), BF16),
        vmem((LOC, SLAB, ROWS * CG), BF16),
        vmem((3, W, CG), BF16),
        vmem((3, W, ROWS * CG), BF16),
        vmem((NPL, W, ROWS * CG), BF16),
        vmem((4, W, W), BF16),
        vmem((W, W), BF16),
        vmem((3, W, ROWS * CG), BF16),
        vmem((LOC, W, CG), F32),
        vmem((LOC, W, CG), BF16),
        vmem((NPL, W, CG), BF16),
        vmem((CG, TOPL * SLAB), BF16),
        vmem((2, ROWS, CP, CG), BF16),
        vmem((CG, 2 * CG), BF16),
        vmem((ROWS, CP, 2 * CG), BF16),
        vmem((3, CP, W), BF16),
        vmem((3, CP, W), BF16),
        vmem((2, CP, W), BF16),
        vmem((3, 2, CP, W), BF16),
        vmem((CG, ROWS * CG), BF16),
        vmem((NPL, W, CG), BF16),
        vmem((NPL, W, CG), BF16),
        vmem((NPL, W, CG), BF16),
        vmem((LOC, SLAB, CG), F32),
        vmem((TOPL, SLAB, CG), F32),
        pltpu.SemaphoreType.DMA((48,)),
        pltpu.SemaphoreType.DMA((200,)),
        pltpu.SemaphoreType.DMA((200,)),
    ]
    return pl.pallas_call(
        kernel,
        out_shape=(
            vmem((LOC, SLAB // COLS, R), F32),
            vmem((1, TOPL, SLAB // COLS, R), F32),
        ),
        in_specs=[pl.BlockSpec(memory_space=pltpu.SMEM)] + [any_space] * 12,
        out_specs=(any_space, any_space),
        scratch_shapes=scratch,
        compiler_params=pltpu.CompilerParams(
            collective_id=0, has_side_effects=True, vmem_limit_bytes=60 * 1024 * 1024
        ),
    )(*arrays)


def solution(mesh):
    placed = (
        P("gz"),
        P("gz", "row", "col"),
        P("gz", None, "row", "col"),
        P(None, None, "row", "col"),
        P("gz", "col", "row"),
        P("gz", None, "col", "row"),
        P(None, None, "col", "row"),
        P("gz", "col", None),
        P(None, "col", None),
        P("gz", "row", None),
        P(None, "row", None),
        P("gz", "row", None),
        P(None, "row", None),
    )
    return jax.shard_map(
        per_device,
        mesh=mesh,
        in_specs=placed,
        out_specs=(P("gz", ("row", "col"), None), P("gz", None, ("row", "col"), None)),
        check_vma=False,
    )
```

```python
import functools

import jax
import jax.numpy as jnp
from jax import lax
from jax.experimental import pallas as pl
from jax.experimental.pallas import tpu as pltpu
from jax.sharding import PartitionSpec as P

F32 = jnp.float32
BF16 = jnp.bfloat16
MESH = pl.DeviceIdType.MESH
ROWS, COLS, LAYERS = 8, 4, 16
NPL, LOC, TOPL = 4, 8, 4
W, R = 256, 512
SLAB, KCH = W // ROWS, W // COLS
CG = R // COLS
CP = CG // ROWS
L_PAIRS = ((0, 1), (0, 2), (0, 3), (1, 2), (1, 3), (2, 3))
Z_BASE = (0, 4, 7, 9)


def nt(a, b):
    return lax.dot_general(a, b, (((1,), (1,)), ((), ())), preferred_element_type=F32)


def mm(a, b):
    return jnp.dot(a, b, preferred_element_type=F32)


def aligned(value, size):
    return pl.ds(pl.multiple_of(value * size, size), size)


def kernel(
    parent, l_tree, l_path, l_top, u_tree, u_path, u_top, linv_local, linv_top, uinv_local,
    uinv_top, rhs_local, rhs_top, x_local, x_path,
    st_ltree, st_lpath, st_ltop, st_utree, st_upath, st_utop, uinv_own, rhs2_own, st_rt,
    x1, linv, lt, lp, ltp1, ltp, linvt, uinvt, uinv2, up, us, utp, ut, tree_w, mprod, vprod, nprod,
    y, ylow, s2f, tt, rv, rt, rr, zs, zr, xp, sb2, x2low, sb1, out_l, out_p,
    lsem, ssem, rsem,
):
    r = lax.axis_index("row")
    c = lax.axis_index("col")
    g = lax.axis_index("gz")
    chip, core = r // 2, lax.rem(r, 2)
    sibling = chip * 2 + 1 - core
    counters = {"l": 0, "s": 0, "r": 0}
    pending_sends = []

    def take(kind, count=1):
        first = counters[kind]
        counters[kind] += count
        return first

    def local(src, dst):
        copy = pltpu.make_async_copy(src, dst, lsem.at[take("l")])
        copy.start()
        return copy

    def remote(src, dst, slot, target):
        copy = pltpu.make_async_remote_copy(
            src_ref=src, dst_ref=dst, send_sem=ssem.at[take("s")], recv_sem=rsem.at[slot],
            device_id=target, device_id_type=MESH,
        )
        copy.start()
        pending_sends.append(copy)

    def drain(keep=0):
        done = len(pending_sends) - keep
        for copy in pending_sends[:done]:
            copy.wait_send()
        del pending_sends[:done]

    def await_slot(dst, slot):
        pltpu.make_async_remote_copy(
            src_ref=dst, dst_ref=dst, send_sem=ssem.at[0], recv_sem=rsem.at[slot],
            device_id={"row": r}, device_id_type=MESH,
        ).wait_recv()

    def spread(axis, src_of, dst_of):
        me, size = (r, ROWS) if axis == "row" else (c, COLS)
        base = take("r", size)
        for step in range(1, size):
            peer = lax.rem(me + step, size)
            remote(src_of(peer), dst_of(me), base + step, {axis: peer})

        def wait():
            for step in range(1, size):
                await_slot(dst_of(lax.rem(me + size - step, size)), base + step)

        return wait

    def row_of(other_chip, other_core):
        return lax.rem(other_chip + 4, 4) * 2 + other_core

    def spread_row_shared(src, dst_of):
        base = take("r", 8)
        for step in range(1, 4):
            remote(src, dst_of(r), base + step, {"row": row_of(chip + step, core)})
        remote(src, dst_of(r), base, {"row": sibling})

        def forward():
            for step in range(1, 4):
                place = dst_of(row_of(chip - step, core))
                await_slot(place, base + step)
                remote(place, place, base + 4 + step, {"row": sibling})

        def wait():
            await_slot(dst_of(sibling), base)
            for step in range(1, 4):
                await_slot(dst_of(row_of(chip - step, 1 - core)), base + 4 + step)

        return forward, wait

    def spread_col_shared(src, dst_of):
        base = take("r", 8)
        for step in range(1, COLS):
            remote(src, dst_of(c, core), base + step, {"col": lax.rem(c + step, COLS)})

        def forward():
            for step in range(1, COLS):
                place = dst_of(lax.rem(c + COLS - step, COLS), core)
                await_slot(place, base + step)
                remote(place, place, base + 4 + step, {"row": sibling})

        def wait():
            for step in range(1, COLS):
                await_slot(dst_of(lax.rem(c + COLS - step, COLS), 1 - core), base + 4 + step)

        return forward, wait

    anc = [LAYERS - (LAYERS >> a) + g // 2 ** (a + 1) for a in range(TOPL)]
    my_rows = aligned(r, SLAB)
    my_k = aligned(c, KCH)
    my_cols = aligned(c, CG)
    half_src = aligned(core, SLAB)

    def half_rows(owner, half):
        return aligned(owner * 2 + half, SLAB)

    def lanes_of(owner):
        return pl.ds(pl.multiple_of(owner * CG, CG), CG)

    c_ltree = local(l_tree, st_ltree)
    c_lpath = local(l_path, st_lpath)
    c_ltop = [local(l_top.at[anc[a]], st_ltop.at[a]) for a in range(3)]

    barrier = pltpu.get_barrier_semaphore()

    def greet(target):
        pl.semaphore_signal(barrier, inc=1, device_id=target, device_id_type=MESH)

    partners = []
    for a in range(TOPL - 1):
        span = 2**a
        partners.append(g + span - 2 * span * lax.rem(g // span, 2))
    quarter = g // 4
    source = jnp.where(quarter == 0, 15, jnp.where(quarter == 1, 8, jnp.where(quarter == 2, 7, 0)))
    edge = jnp.logical_or(jnp.logical_or(g == 0, g == 7), jnp.logical_or(g == 8, g == 15))
    first_target = jnp.where(g == 0, 12, jnp.where(g == 7, 8, jnp.where(g == 8, 4, 0)))
    greet({"gz": source})
    greet({"gz": partners[2]})
    greet({"gz": partners[1]})
    for step in range(ROWS):
        greet({"row": lax.rem(r + step, ROWS), "gz": partners[0]})
    for step in range(1, ROWS):
        greet({"row": lax.rem(r + step, ROWS)})
    for step in range(1, COLS):
        greet({"col": lax.rem(c + step, COLS)})

    pl.semaphore_wait(barrier, ROWS - 1 + ROWS + COLS - 1 + 2 + jnp.where(edge, 4, 0))

    w_x1 = spread(
        "row", lambda peer: rhs_local.at[pl.ds(0, NPL), :, my_cols],
        lambda me: x1.at[:, aligned(me, SLAB), :],
    )
    f_li1, w_li1 = spread_col_shared(
        linv_local.at[pl.ds(0, NPL), half_src], lambda o, h: linv.at[pl.ds(0, NPL), half_rows(o, h), :]
    )
    c_x1 = local(rhs_local.at[pl.ds(0, NPL), :, my_cols], x1.at[:, my_rows, :])
    c_li1 = local(linv_local.at[pl.ds(0, NPL)], linv.at[pl.ds(0, NPL), my_k, :])
    c_lit = [local(linv_top.at[anc[a]], linvt.at[a, my_k, :]) for a in range(TOPL)]
    c_uit = [local(uinv_top.at[anc[a]], uinvt.at[a, my_rows, :]) for a in range(TOPL)]
    c_rt = [local(rhs_top.at[anc[a], :, my_cols], st_rt.at[a]) for a in range(TOPL)]
    c_li2 = local(linv_local.at[pl.ds(NPL, NPL)], linv.at[pl.ds(NPL, NPL), my_k, :])
    c_rhs2 = local(rhs_local.at[pl.ds(NPL, NPL), :, my_cols], rhs2_own)
    c_utop = [local(u_top.at[anc[a]], st_utop.at[a]) for a in range(3)]
    c_utree = local(u_tree, st_utree)
    c_upath = local(u_path, st_upath)
    c_ui2 = local(uinv_local.at[pl.ds(NPL, NPL)], uinv2.at[:, my_rows, :])
    c_uiown = local(uinv_local, uinv_own)

    c_ltree.wait()
    for b in range(NPL // 2):
        lt[c, b] = jnp.concatenate([st_ltree[2 * b], st_ltree[2 * b + 1]], axis=-1)
    w_lt = spread("col", lambda peer: lt.at[c], lambda me: lt.at[me])
    for copy in c_ltop:
        copy.wait()
    for b in range(len(L_PAIRS) // 2):
        (a1, m1), (a2, m2) = L_PAIRS[2 * b], L_PAIRS[2 * b + 1]
        ltp1[c, b] = jnp.concatenate([st_ltop[a1, m1], st_ltop[a2, m2]], axis=-1)
    w_ltp1 = spread("col", lambda peer: ltp1.at[c], lambda me: ltp1.at[me])
    f_li2, w_li2 = spread_col_shared(
        linv_local.at[pl.ds(NPL, NPL), half_src], lambda o, h: linv.at[pl.ds(NPL, NPL), half_rows(o, h), :]
    )
    c_lpath.wait()
    for m in range(TOPL):
        lp[c, pl.ds(m * SLAB, SLAB), :] = jnp.concatenate([st_lpath[k, m] for k in range(LOC)], axis=-1)
    w_lp = spread("col", lambda peer: lp.at[c], lambda me: lp.at[me])

    def unpaired(pieces, b):
        half = pl.ds(b % 2 * KCH, KCH)
        return jnp.concatenate([pieces[q, b // 2, :, half] for q in range(COLS)], axis=-1)

    for copy in c_lit:
        copy.wait()
    f_lit, w_lit = spread_col_shared(
        linvt.at[:, half_rows(c, core), :], lambda o, h: linvt.at[:, half_rows(o, h), :]
    )
    for copy in c_uit:
        copy.wait()
    f_uit, w_uit = spread_row_shared(uinvt.at[:, my_rows, :], lambda me: uinvt.at[:, aligned(me, SLAB), :])

    c_ui2.wait()
    f_ui2, w_ui2 = spread_row_shared(uinv2.at[:, my_rows, :], lambda me: uinv2.at[:, aligned(me, SLAB), :])

    c_x1.wait()
    c_li1.wait()
    f_li1()
    w_x1()
    w_li1()
    for j in range(NPL):
        solved = mm(linv[j], x1[j])
        y[j] = solved
        ylow[j] = solved.astype(BF16)
    w_lt()
    terms = []
    for j in range(NPL):
        terms.append(mm(unpaired(lt, j), ylow[j]))
    c_rhs2.wait()
    for i in range(NPL):
        value = rhs2_own[i].astype(F32)
        for j in range(NPL):
            value = value - jnp.where(parent[j] == i, 1.0, 0.0).astype(F32) * terms[j]
        s2f[i, my_rows, :] = value.astype(BF16)
    w_s2 = spread("row", lambda peer: s2f.at[:, my_rows, :], lambda me: s2f.at[:, aligned(me, SLAB), :])

    eye = (
        lax.broadcasted_iota(jnp.int32, (CG, CG), 0) == lax.broadcasted_iota(jnp.int32, (CG, CG), 1)
    ).astype(F32).astype(BF16)
    for copy in c_rt:
        copy.wait()
    rt[...] = nt(eye, st_rt[...].reshape(TOPL * SLAB, CG)).astype(BF16)
    w_rr = spread("row", lambda peer: rt.at[aligned(peer, CP), :], lambda me: rr.at[me])
    rr[r] = rt[aligned(r, CP), :]
    w_ltp1()
    for b in range(len(L_PAIRS)):
        ltp[b, my_rows, :] = unpaired(ltp1, b)
    f_ltp, w_ltp = spread_row_shared(ltp.at[:, my_rows, :], lambda me: ltp.at[:, aligned(me, SLAB), :])
    f_li2()

    eye_k = eye[0:KCH, 0:KCH]

    def packed(stack):
        return nt(eye_k, stack).astype(BF16)

    for copy in c_utop:
        copy.wait()
    utp[0, my_k, :] = packed(jnp.concatenate([st_utop[2, 3], st_utop[0, 1], st_utop[0, 2], st_utop[0, 3]], axis=0))
    utp[1, my_k, :] = packed(st_utop[1].reshape(CG, KCH))
    c_utree.wait()
    utp[2, my_k, :] = packed(st_utree[...].reshape(CG, KCH))
    w_utp = spread("col", lambda peer: utp.at[:, my_k, :], lambda me: utp.at[:, aligned(me, KCH), :])
    c_upath.wait()
    for k in range(LOC):
        up[k, my_k, :] = packed(st_upath[k].reshape(CG, KCH))

    w_up = spread("col", lambda peer: up.at[:, my_k, :], lambda me: up.at[:, aligned(me, KCH), :])
    w_lp()
    toward = jnp.zeros((TOPL * SLAB, CG), F32)
    for q in range(COLS):
        block = ylow[0:NPL, q * KCH:(q + 1) * KCH, :].reshape(NPL * KCH, CG)
        toward = toward + mm(lp[q, :, 0:NPL * KCH], block)

    c_li2.wait()
    w_li2()
    w_s2()
    for i in range(NPL):
        solved = mm(linv[NPL + i], s2f[i])
        y[NPL + i] = solved
        ylow[NPL + i] = solved.astype(BF16)
    for q in range(COLS):
        block = ylow[NPL:LOC, q * KCH:(q + 1) * KCH, :].reshape(NPL * KCH, CG)
        toward = toward + mm(lp[q, :, NPL * KCH:LOC * KCH], block)
    tt[...] = nt(eye, toward.astype(BF16)).astype(BF16)
    base = take("r", 2 * ROWS)
    remote(tt.at[aligned(r, CP), :], rv.at[1, r], base + ROWS, {"gz": partners[0]})
    for step in range(1, ROWS):
        peer = lax.rem(r + step, ROWS)
        remote(tt.at[aligned(peer, CP), :], rv.at[1, r], base + ROWS + step, {"row": peer, "gz": partners[0]})
        remote(tt.at[aligned(peer, CP), :], rv.at[0, r], base + step, {"row": peer})
    rv[0, r] = tt[aligned(r, CP), :]

    def w_rv():
        await_slot(rv.at[1, r], base + ROWS)
        for step in range(1, ROWS):
            sender = lax.rem(r + ROWS - step, ROWS)
            await_slot(rv.at[0, sender], base + step)
            await_slot(rv.at[1, sender], base + ROWS + step)

    f_lit()

    slot_of_lane = lax.shift_right_logical(lax.broadcasted_iota(jnp.int32, (CP, CG), 1), 5)

    def by_level(tiles, m):
        halves = []
        for q in range(2):
            total = None
            for s in range(4):
                piece = tiles[4 * q + s]
                if s != m:
                    piece = pltpu.roll(piece, (s - m) * SLAB % CG, 1)
                total = piece if total is None else jnp.where(slot_of_lane == s, piece, total)
            halves.append(total)
        return jnp.concatenate(halves, axis=-1)

    w_rr()
    rr_tiles = [rr[q].astype(F32) for q in range(ROWS)]
    top_rhs = [by_level(rr_tiles, m) for m in range(TOPL)]
    w_utp()
    f_ut, w_ut = spread_row_shared(utp, lambda me: ut.at[:, :, lanes_of(me)])
    c_ut = local(utp, ut.at[:, :, lanes_of(r)])
    f_ltp()
    w_rv()
    rv_tiles = [rv[0, q].astype(F32) + rv[1, q].astype(F32) for q in range(ROWS)]
    pend = [by_level(rv_tiles, m) for m in range(TOPL)]
    w_lit()
    w_ltp()

    top_y = []
    for a in range(TOPL):
        count = TOPL - a
        base = Z_BASE[a]
        if a > 0:
            place = pl.ds(base, count)
            for m in range(a, TOPL):
                zs[base + m - a] = pend[m].astype(BF16)
            slot = take("r")
            if a < TOPL - 1:
                remote(zs.at[place], zr.at[place], slot, {"gz": partners[a]})
            else:
                last_sends = [
                    pltpu.make_async_remote_copy(
                        src_ref=zs.at[place], dst_ref=zr.at[place], send_sem=ssem.at[take("s")],
                        recv_sem=rsem.at[slot], device_id={"gz": first_target + step}, device_id_type=MESH,
                    )
                    for step in range(4)
                ]

                @pl.when(edge)
                def _():
                    for copy in last_sends:
                        copy.start()

            if a == 1:
                f_uit()
                f_ui2()
                for n, (b, below) in enumerate(((3, 1), (4, 1), (5, 2))):
                    mprod[n] = mm(ltp[b], linvt[below]).astype(BF16)
            if a == 2:
                w_up()
                w_us = spread(
                    "row", lambda peer: up.at[:, aligned(peer, SLAB), :], lambda me: us.at[:, :, lanes_of(me)]
                )
                c_us = local(up.at[:, my_rows, :], us.at[:, :, lanes_of(r)])
                w_uit()
                vprod[...] = mm(uinvt[TOPL - 1], linvt[TOPL - 1]).astype(BF16)
                known_x = [nt(top_y[n].astype(BF16), uinvt[n]) for n in range(2)]
            if a == 3:
                known_x.append(nt(top_y[2].astype(BF16), uinvt[2]))
                f_ut()
                c_ut.wait()
                w_ut()
                for n, tile in enumerate((0, 1, 0)):
                    nprod[n] = mm(uinvt[n], ut[tile]).astype(BF16)
            await_slot(zr.at[place], slot)
            for m in range(a, TOPL):
                pend[m] = pend[m] + zr[base + m - a].astype(F32)
        low = (top_rhs[a] - pend[a]).astype(BF16)
        if a == 0:
            top_y.append(nt(low, linvt[a]))
            low = top_y[0].astype(BF16)
            for b in range(3):
                pend[b + 1] = pend[b + 1] + nt(low, ltp[b])
        elif a < TOPL - 1:
            for m in range(a + 1, TOPL):
                pend[m] = pend[m] + nt(low, mprod[m - 2 if a == 1 else 2])
            top_y.append(nt(low, linvt[a]))
        else:
            known_x.append(nt(low, vprod[...]))

    tiles = [jnp.zeros((CP, CG), F32) for _ in range(ROWS)]
    for a in reversed(range(TOPL)):
        solved = known_x[a]
        if a < TOPL - 1:
            if a == 2:
                known = [pltpu.roll(tile, SLAB, 1) for tile in tiles]
            else:
                known = tiles
            above = jnp.concatenate(known, axis=-1).astype(BF16)
            solved = solved - nt(above, nprod[a])
        for q in range(2):
            half = solved[:, q * CG:(q + 1) * CG]
            for s in range(4):
                piece = half if a == s else pltpu.roll(half, (a - s) * SLAB % CG, 1)
                tiles[4 * q + s] = jnp.where(slot_of_lane == a, piece, tiles[4 * q + s])
    my_cp = aligned(r, CP)
    xp[my_cp, :] = jnp.concatenate(tiles, axis=-1).astype(BF16)
    w_xp = spread("row", lambda peer: xp.at[my_cp, :], lambda me: xp.at[aligned(me, CP), :])

    lane_slot = lax.shift_right_logical(lax.broadcasted_iota(jnp.int32, (8, CG), 1), 5)
    for j in range(NPL):
        mask = jnp.where(lane_slot == j, 1.0, 0.0).astype(F32)[0:1, :].astype(BF16)
        for q in range(ROWS):
            tree_w[j, :, q * CG:(q + 1) * CG] = ut[2, :, q * CG:(q + 1) * CG] * mask
    c_us.wait()
    w_us()
    w_xp()
    path = xp[...]
    path_term2 = nt(us[NPL:LOC].reshape(NPL * SLAB, ROWS * CG), path)
    for i in range(NPL):
        value = y[NPL + i, my_rows, :] - path_term2[i * SLAB:(i + 1) * SLAB, :]
        sb2[i, my_rows, :] = value.astype(BF16)
    f_sb2, w_sb2 = spread_row_shared(sb2.at[:, my_rows, :], lambda me: sb2.at[:, aligned(me, SLAB), :])
    path_term1 = nt(us[0:NPL].reshape(NPL * SLAB, ROWS * CG), path)
    for j in range(NPL):
        value = y[j, my_rows, :] - path_term1[j * SLAB:(j + 1) * SLAB, :]
        sb1[j, my_rows, :] = value.astype(BF16)
    f_sb1, w_sb1 = spread_row_shared(sb1.at[:, my_rows, :], lambda me: sb1.at[:, aligned(me, SLAB), :])
    own_path = nt(eye, xp[:, lanes_of(r)])
    for m in range(TOPL):
        out_p[m] = own_path[m * SLAB:(m + 1) * SLAB, :]
    piece_rows = SLAB // COLS

    def out_rows(peer):
        return pl.ds(pl.multiple_of(peer * piece_rows, piece_rows), piece_rows)

    w_outp = spread(
        "col", lambda peer: out_p.at[:, out_rows(peer), :], lambda me: x_path.at[0, :, :, lanes_of(me)]
    )
    c_outp = local(out_p.at[:, out_rows(c), :], x_path.at[0, :, :, my_cols])

    w_ui2()
    c_uiown.wait()
    drain(14)

    @pl.when(edge)
    def _():
        for copy in last_sends:
            copy.wait_send()

    f_sb2()
    f_sb1()
    w_sb2()
    for i in range(NPL):
        x2low[i] = mm(uinv2[i], sb2[i]).astype(BF16)
    parent_x = [x2low[parent[j]].reshape(ROWS, 1, SLAB, CG) for j in range(NPL)]
    stacked = jnp.concatenate(parent_x, axis=1).reshape(ROWS * NPL * SLAB, CG)
    trees = [mm(tree_w[j], stacked) for j in range(NPL)]
    for i in range(NPL):
        out_l[NPL + i] = mm(uinv_own[NPL + i], sb2[i])

    def send_out(first):
        part = pl.ds(first, NPL)
        wait = spread(
            "col", lambda peer: out_l.at[part, out_rows(peer), :], lambda me: x_local.at[part, :, lanes_of(me)]
        )
        return wait, local(out_l.at[part, out_rows(c), :], x_local.at[part, :, my_cols])

    w_out2, c_out2 = send_out(NPL)
    w_sb1()
    for j in range(NPL):
        out_l[j] = mm(uinv_own[j], (sb1[j].astype(F32) - trees[j]).astype(BF16))
    w_out1, c_out1 = send_out(0)
    w_outp()
    w_out2()
    c_outp.wait()
    c_out2.wait()
    drain(COLS - 1)
    w_out1()
    c_out1.wait()
    drain()


def per_device(*arrays):
    arrays = list(arrays)
    for index in (4, 5, 6):
        arrays[index] = jnp.swapaxes(arrays[index], -1, -2)
    any_space = pl.BlockSpec(memory_space=pl.ANY)
    vmem = pltpu.VMEM
    scratch = [
        vmem((NPL, SLAB, KCH), BF16),
        vmem((LOC, TOPL, SLAB, KCH), BF16),
        vmem((3, TOPL, SLAB, KCH), BF16),
        vmem((NPL, SLAB, KCH), BF16),
        vmem((LOC, TOPL, SLAB, KCH), BF16),
        vmem((3, TOPL, SLAB, KCH), BF16),
        vmem((LOC, SLAB, W), BF16),
        vmem((NPL, SLAB, CG), BF16),
        vmem((TOPL, SLAB, CG), BF16),
        vmem((NPL, W, CG), BF16),
        vmem((LOC, W, W), BF16),
        vmem((COLS, NPL // 2, SLAB, CG), BF16),
        vmem((COLS, TOPL * SLAB, LOC * KCH), BF16),
        vmem((COLS, 3, SLAB, CG), BF16),
        vmem((6, W, W), BF16),
        vmem((TOPL, W, W), BF16),
        vmem((TOPL, W, W), BF16),
        vmem((NPL, W, W), BF16),
        vmem((LOC, W, CG), BF16),
        vmem((LOC, SLAB, ROWS * CG), BF16),
        vmem((3, W, CG), BF16),
        vmem((3, W, ROWS * CG), BF16),
        vmem((NPL, W, ROWS * CG), BF16),
        vmem((3, W, W), BF16),
        vmem((W, W), BF16),
        vmem((3, W, ROWS * CG), BF16),
        vmem((LOC, W, CG), F32),
        vmem((LOC, W, CG), BF16),
        vmem((NPL, W, CG), BF16),
        vmem((CG, TOPL * SLAB), BF16),
        vmem((2, ROWS, CP, CG), BF16),
        vmem((CG, TOPL * SLAB), BF16),
        vmem((ROWS, CP, CG), BF16),
        vmem((10, CP, W), BF16),
        vmem((10, CP, W), BF16),
        vmem((CG, ROWS * CG), BF16),
        vmem((NPL, W, CG), BF16),
        vmem((NPL, W, CG), BF16),
        vmem((NPL, W, CG), BF16),
        vmem((LOC, SLAB, CG), F32),
        vmem((TOPL, SLAB, CG), F32),
        pltpu.SemaphoreType.DMA((48,)),
        pltpu.SemaphoreType.DMA((200,)),
        pltpu.SemaphoreType.DMA((200,)),
    ]
    return pl.pallas_call(
        kernel,
        out_shape=(
            vmem((LOC, SLAB // COLS, R), F32),
            vmem((1, TOPL, SLAB // COLS, R), F32),
        ),
        in_specs=[pl.BlockSpec(memory_space=pltpu.SMEM)] + [any_space] * 12,
        out_specs=(any_space, any_space),
        scratch_shapes=scratch,
        compiler_params=pltpu.CompilerParams(
            collective_id=0, has_side_effects=True, vmem_limit_bytes=60 * 1024 * 1024
        ),
    )(*arrays)


def solution(mesh):
    placed = (
        P("gz"),
        P("gz", "row", "col"),
        P("gz", None, "row", "col"),
        P(None, None, "row", "col"),
        P("gz", "col", "row"),
        P("gz", None, "col", "row"),
        P(None, None, "col", "row"),
        P("gz", "col", None),
        P(None, "col", None),
        P("gz", "row", None),
        P(None, "row", None),
        P("gz", "row", None),
        P(None, "row", None),
    )
    return jax.shard_map(
        per_device,
        mesh=mesh,
        in_specs=placed,
        out_specs=(P("gz", ("row", "col"), None), P("gz", None, ("row", "col"), None)),
        check_vma=False,
    )
```

```python
import functools

import jax
import jax.numpy as jnp
from jax import lax
from jax.experimental import pallas as pl
from jax.experimental.pallas import tpu as pltpu
from jax.sharding import PartitionSpec as P

F32 = jnp.float32
BF16 = jnp.bfloat16
MESH = pl.DeviceIdType.MESH
ROWS, COLS, LAYERS = 8, 4, 16
NPL, LOC, TOPL = 4, 8, 4
W, R = 256, 512
SLAB, KCH = W // ROWS, W // COLS
CG = R // COLS
CP = CG // ROWS
L_PAIRS = ((0, 1), (0, 2), (0, 3), (1, 2), (1, 3), (2, 3))
Z_BASE = (0, 4, 7, 9)
FAR_FIRST = {8: (4, 3, 5, 2, 6, 1, 7), 4: (2, 1, 3)}


def nt(a, b):
    return lax.dot_general(a, b, (((1,), (1,)), ((), ())), preferred_element_type=F32)


def mm(a, b):
    return jnp.dot(a, b, preferred_element_type=F32)


def aligned(value, size):
    return pl.ds(pl.multiple_of(value * size, size), size)


def kernel(
    parent, l_tree, l_path, l_top, u_tree, u_path, u_top, linv_local, linv_top, uinv_local,
    uinv_top, rhs_local, rhs_top, x_local, x_path,
    st_ltree, st_lpath, st_ltop, st_utree, st_upath, st_utop, uinv_own, rhs2_own, st_rt,
    x1, linv, lt, lp, ltp1, ltp, linvt, uinvt, uinv2, up, us, utp, ut, tree_w, mprod, vprod, nprod,
    y, ylow, s2f, tt, rv, rt, rr, zs, zr, xp, sb2, x2low, sb1, out_l, out_p,
    lsem, ssem, rsem,
):
    r = lax.axis_index("row")
    c = lax.axis_index("col")
    g = lax.axis_index("gz")
    chip, core = r // 2, lax.rem(r, 2)
    sibling = chip * 2 + 1 - core
    counters = {"l": 0, "s": 0, "r": 0}
    pending_sends = []

    def take(kind, count=1):
        first = counters[kind]
        counters[kind] += count
        return first

    def local(src, dst):
        copy = pltpu.make_async_copy(src, dst, lsem.at[take("l")])
        copy.start()
        return copy

    def remote(src, dst, slot, target):
        copy = pltpu.make_async_remote_copy(
            src_ref=src, dst_ref=dst, send_sem=ssem.at[take("s")], recv_sem=rsem.at[slot],
            device_id=target, device_id_type=MESH,
        )
        copy.start()
        pending_sends.append(copy)

    def drain(keep=0):
        done = len(pending_sends) - keep
        for copy in pending_sends[:done]:
            copy.wait_send()
        del pending_sends[:done]

    def await_slot(dst, slot):
        pltpu.make_async_remote_copy(
            src_ref=dst, dst_ref=dst, send_sem=ssem.at[0], recv_sem=rsem.at[slot],
            device_id={"row": r}, device_id_type=MESH,
        ).wait_recv()

    def spread(axis, src_of, dst_of):
        me, size = (r, ROWS) if axis == "row" else (c, COLS)
        base = take("r", size)
        for step in FAR_FIRST[size]:
            peer = lax.rem(me + step, size)
            remote(src_of(peer), dst_of(me), base + step, {axis: peer})

        def wait():
            for step in range(1, size):
                await_slot(dst_of(lax.rem(me + size - step, size)), base + step)

        return wait

    def row_of(other_chip, other_core):
        return lax.rem(other_chip + 4, 4) * 2 + other_core

    def spread_row_shared(src, dst_of):
        base = take("r", 8)
        for step in range(1, 4):
            remote(src, dst_of(r), base + step, {"row": row_of(chip + step, core)})
        remote(src, dst_of(r), base, {"row": sibling})

        def forward():
            for step in range(1, 4):
                place = dst_of(row_of(chip - step, core))
                await_slot(place, base + step)
                remote(place, place, base + 4 + step, {"row": sibling})

        def wait():
            await_slot(dst_of(sibling), base)
            for step in range(1, 4):
                await_slot(dst_of(row_of(chip - step, 1 - core)), base + 4 + step)

        return forward, wait

    def spread_col_shared(src, dst_of):
        base = take("r", 8)
        for step in range(1, COLS):
            remote(src, dst_of(c, core), base + step, {"col": lax.rem(c + step, COLS)})

        def forward():
            for step in range(1, COLS):
                place = dst_of(lax.rem(c + COLS - step, COLS), core)
                await_slot(place, base + step)
                remote(place, place, base + 4 + step, {"row": sibling})

        def wait():
            for step in range(1, COLS):
                await_slot(dst_of(lax.rem(c + COLS - step, COLS), 1 - core), base + 4 + step)

        return forward, wait

    anc = [LAYERS - (LAYERS >> a) + g // 2 ** (a + 1) for a in range(TOPL)]
    my_rows = aligned(r, SLAB)
    my_k = aligned(c, KCH)
    my_cols = aligned(c, CG)
    half_src = aligned(core, SLAB)

    def half_rows(owner, half):
        return aligned(owner * 2 + half, SLAB)

    def lanes_of(owner):
        return pl.ds(pl.multiple_of(owner * CG, CG), CG)


    barrier = pltpu.get_barrier_semaphore()

    def greet(target):
        pl.semaphore_signal(barrier, inc=1, device_id=target, device_id_type=MESH)

    partners = []
    for a in range(TOPL - 1):
        span = 2**a
        partners.append(g + span - 2 * span * lax.rem(g // span, 2))
    quarter = g // 4
    source = jnp.where(quarter == 0, 15, jnp.where(quarter == 1, 8, jnp.where(quarter == 2, 7, 0)))
    edge = jnp.logical_or(jnp.logical_or(g == 0, g == 7), jnp.logical_or(g == 8, g == 15))
    first_target = jnp.where(g == 0, 12, jnp.where(g == 7, 8, jnp.where(g == 8, 4, 0)))
    for step in range(1, COLS):
        greet({"col": lax.rem(c + step, COLS)})
    for step in range(1, ROWS):
        greet({"row": lax.rem(r + step, ROWS)})
    greet({"gz": source})
    greet({"gz": partners[2]})
    greet({"gz": partners[1]})
    for step in range(ROWS):
        greet({"row": lax.rem(r + step, ROWS), "gz": partners[0]})

    c_ltree = local(l_tree, st_ltree)
    c_lpath = local(l_path, st_lpath)
    c_ltop = [local(l_top.at[anc[a]], st_ltop.at[a]) for a in range(3)]

    pl.semaphore_wait(barrier, ROWS - 1 + ROWS + COLS - 1 + 2 + jnp.where(edge, 4, 0))

    w_x1 = spread(
        "row", lambda peer: rhs_local.at[pl.ds(0, NPL), :, my_cols],
        lambda me: x1.at[:, aligned(me, SLAB), :],
    )
    f_li1, w_li1 = spread_col_shared(
        linv_local.at[pl.ds(0, NPL), half_src], lambda o, h: linv.at[pl.ds(0, NPL), half_rows(o, h), :]
    )
    c_x1 = local(rhs_local.at[pl.ds(0, NPL), :, my_cols], x1.at[:, my_rows, :])
    c_li1 = local(linv_local.at[pl.ds(0, NPL)], linv.at[pl.ds(0, NPL), my_k, :])
    c_lit = [local(linv_top.at[anc[a]], linvt.at[a, my_k, :]) for a in range(TOPL)]
    c_uit = [local(uinv_top.at[anc[a]], uinvt.at[a, my_rows, :]) for a in range(TOPL)]
    c_rt = [local(rhs_top.at[anc[a], :, my_cols], st_rt.at[a]) for a in range(TOPL)]
    c_li2 = local(linv_local.at[pl.ds(NPL, NPL)], linv.at[pl.ds(NPL, NPL), my_k, :])
    c_rhs2 = local(rhs_local.at[pl.ds(NPL, NPL), :, my_cols], rhs2_own)
    c_utop = [local(u_top.at[anc[a]], st_utop.at[a]) for a in range(3)]
    c_utree = local(u_tree, st_utree)
    c_upath = local(u_path, st_upath)
    c_ui2 = local(uinv_local.at[pl.ds(NPL, NPL)], uinv2.at[:, my_rows, :])
    c_uiown = local(uinv_local, uinv_own)

    c_ltree.wait()
    for b in range(NPL // 2):
        lt[c, b] = jnp.concatenate([st_ltree[2 * b], st_ltree[2 * b + 1]], axis=-1)
    w_lt = spread("col", lambda peer: lt.at[c], lambda me: lt.at[me])
    for copy in c_ltop:
        copy.wait()
    for b in range(len(L_PAIRS) // 2):
        (a1, m1), (a2, m2) = L_PAIRS[2 * b], L_PAIRS[2 * b + 1]
        ltp1[c, b] = jnp.concatenate([st_ltop[a1, m1], st_ltop[a2, m2]], axis=-1)
    w_ltp1a = spread("col", lambda peer: ltp1.at[c, pl.ds(0, 2)], lambda me: ltp1.at[me, pl.ds(0, 2)])
    f_li2, w_li2 = spread_col_shared(
        linv_local.at[pl.ds(NPL, NPL), half_src], lambda o, h: linv.at[pl.ds(NPL, NPL), half_rows(o, h), :]
    )
    c_lpath.wait()
    for m in range(TOPL):
        lp[c, pl.ds(m * SLAB, SLAB), :] = jnp.concatenate([st_lpath[k, m] for k in range(LOC)], axis=-1)
    w_lp = spread("col", lambda peer: lp.at[c], lambda me: lp.at[me])

    def unpaired(pieces, b):
        half = pl.ds(b % 2 * KCH, KCH)
        return jnp.concatenate([pieces[q, b // 2, :, half] for q in range(COLS)], axis=-1)

    for copy in c_lit:
        copy.wait()
    first, rest = pl.ds(0, 1), pl.ds(1, TOPL - 1)
    f_lit0, w_lit0 = spread_col_shared(
        linvt.at[first, half_rows(c, core), :], lambda o, h: linvt.at[first, half_rows(o, h), :]
    )
    w_ltp1b = spread("col", lambda peer: ltp1.at[c, pl.ds(2, 1)], lambda me: ltp1.at[me, pl.ds(2, 1)])
    f_lit, w_lit = spread_col_shared(
        linvt.at[rest, half_rows(c, core), :], lambda o, h: linvt.at[rest, half_rows(o, h), :]
    )
    for copy in c_uit:
        copy.wait()
    f_uit, w_uit = spread_row_shared(uinvt.at[:, my_rows, :], lambda me: uinvt.at[:, aligned(me, SLAB), :])

    c_ui2.wait()
    f_ui2, w_ui2 = spread_row_shared(uinv2.at[:, my_rows, :], lambda me: uinv2.at[:, aligned(me, SLAB), :])

    c_x1.wait()
    c_li1.wait()
    f_li1()
    w_x1()
    w_li1()
    for j in range(NPL):
        solved = mm(linv[j], x1[j])
        y[j] = solved
        ylow[j] = solved.astype(BF16)
    w_lt()
    terms = []
    for j in range(NPL):
        terms.append(mm(unpaired(lt, j), ylow[j]))
    c_rhs2.wait()
    for i in range(NPL):
        value = rhs2_own[i].astype(F32)
        for j in range(NPL):
            value = value - jnp.where(parent[j] == i, 1.0, 0.0).astype(F32) * terms[j]
        s2f[i, my_rows, :] = value.astype(BF16)
    w_s2 = spread("row", lambda peer: s2f.at[:, my_rows, :], lambda me: s2f.at[:, aligned(me, SLAB), :])

    eye = (
        lax.broadcasted_iota(jnp.int32, (CG, CG), 0) == lax.broadcasted_iota(jnp.int32, (CG, CG), 1)
    ).astype(F32).astype(BF16)
    for copy in c_rt:
        copy.wait()
    rt[...] = nt(eye, st_rt[...].reshape(TOPL * SLAB, CG)).astype(BF16)
    w_rr = spread("row", lambda peer: rt.at[aligned(peer, CP), :], lambda me: rr.at[me])
    rr[r] = rt[aligned(r, CP), :]
    w_ltp1a()
    for b in range(4):
        ltp[b, my_rows, :] = unpaired(ltp1, b)
    lower, upper = pl.ds(0, 3), pl.ds(3, 3)
    f_ltpa, w_ltpa = spread_row_shared(
        ltp.at[lower, my_rows, :], lambda me: ltp.at[lower, aligned(me, SLAB), :]
    )
    f_li2()

    eye_k = eye[0:KCH, 0:KCH]

    def packed(stack):
        return nt(eye_k, stack).astype(BF16)

    for copy in c_utop:
        copy.wait()
    utp[0, my_k, :] = packed(jnp.concatenate([st_utop[2, 3], st_utop[0, 1], st_utop[0, 2], st_utop[0, 3]], axis=0))
    utp[1, my_k, :] = packed(st_utop[1].reshape(CG, KCH))
    c_utree.wait()
    utp[2, my_k, :] = packed(st_utree[...].reshape(CG, KCH))
    w_utp = spread("col", lambda peer: utp.at[:, my_k, :], lambda me: utp.at[:, aligned(me, KCH), :])
    c_upath.wait()
    for k in range(LOC):
        up[k, my_k, :] = packed(st_upath[k].reshape(CG, KCH))

    w_up = spread("col", lambda peer: up.at[:, my_k, :], lambda me: up.at[:, aligned(me, KCH), :])
    w_lp()
    toward = jnp.zeros((TOPL * SLAB, CG), F32)
    for q in range(COLS):
        block = ylow[0:NPL, q * KCH:(q + 1) * KCH, :].reshape(NPL * KCH, CG)
        toward = toward + mm(lp[q, :, 0:NPL * KCH], block)

    c_li2.wait()
    w_li2()
    w_s2()
    for i in range(NPL):
        solved = mm(linv[NPL + i], s2f[i])
        y[NPL + i] = solved
        ylow[NPL + i] = solved.astype(BF16)
    for q in range(COLS):
        block = ylow[NPL:LOC, q * KCH:(q + 1) * KCH, :].reshape(NPL * KCH, CG)
        toward = toward + mm(lp[q, :, NPL * KCH:LOC * KCH], block)
    tt[...] = nt(eye, toward.astype(BF16)).astype(BF16)
    base = take("r", 2 * ROWS)
    for step in FAR_FIRST[ROWS]:
        peer = lax.rem(r + step, ROWS)
        remote(tt.at[aligned(peer, CP), :], rv.at[1, r], base + ROWS + step, {"row": peer, "gz": partners[0]})
        remote(tt.at[aligned(peer, CP), :], rv.at[0, r], base + step, {"row": peer})
    remote(tt.at[aligned(r, CP), :], rv.at[1, r], base + ROWS, {"gz": partners[0]})
    rv[0, r] = tt[aligned(r, CP), :]

    def w_rv():
        await_slot(rv.at[1, r], base + ROWS)
        for step in range(1, ROWS):
            sender = lax.rem(r + ROWS - step, ROWS)
            await_slot(rv.at[0, sender], base + step)
            await_slot(rv.at[1, sender], base + ROWS + step)

    f_lit0()
    w_ltp1b()
    for b in range(4, 6):
        ltp[b, my_rows, :] = unpaired(ltp1, b)
    f_ltpb, w_ltpb = spread_row_shared(
        ltp.at[upper, my_rows, :], lambda me: ltp.at[upper, aligned(me, SLAB), :]
    )

    slot_of_lane = lax.shift_right_logical(lax.broadcasted_iota(jnp.int32, (CP, CG), 1), 5)

    def by_level(tiles, m):
        halves = []
        for q in range(2):
            total = None
            for s in range(4):
                piece = tiles[4 * q + s]
                if s != m:
                    piece = pltpu.roll(piece, (s - m) * SLAB % CG, 1)
                total = piece if total is None else jnp.where(slot_of_lane == s, piece, total)
            halves.append(total)
        return jnp.concatenate(halves, axis=-1)

    w_rr()
    rr_tiles = [rr[q].astype(F32) for q in range(ROWS)]
    top_rhs = [by_level(rr_tiles, m) for m in range(TOPL)]
    w_utp()
    f_ut, w_ut = spread_row_shared(utp, lambda me: ut.at[:, :, lanes_of(me)])
    c_ut = local(utp, ut.at[:, :, lanes_of(r)])
    f_ltpa()
    w_rv()
    rv_tiles = [rv[0, q].astype(F32) + rv[1, q].astype(F32) for q in range(ROWS)]
    pend = [by_level(rv_tiles, m) for m in range(TOPL)]
    w_lit0()
    w_ltpa()

    top_y = []
    for a in range(TOPL):
        count = TOPL - a
        base = Z_BASE[a]
        if a > 0:
            place = pl.ds(base, count)
            for m in range(a, TOPL):
                zs[base + m - a] = pend[m].astype(BF16)
            slot = take("r")
            if a < TOPL - 1:
                remote(zs.at[place], zr.at[place], slot, {"gz": partners[a]})
            else:
                last_sends = [
                    pltpu.make_async_remote_copy(
                        src_ref=zs.at[place], dst_ref=zr.at[place], send_sem=ssem.at[take("s")],
                        recv_sem=rsem.at[slot], device_id={"gz": first_target + step}, device_id_type=MESH,
                    )
                    for step in range(4)
                ]

                @pl.when(edge)
                def _():
                    for copy in last_sends:
                        copy.start()

            if a == 1:
                f_lit()
                f_ltpb()
                f_uit()
                f_ui2()
                w_lit()
                w_ltpb()
                for n, (b, below) in enumerate(((3, 1), (4, 1), (5, 2))):
                    mprod[n] = mm(ltp[b], linvt[below]).astype(BF16)
            if a == 2:
                w_up()
                w_us = spread(
                    "row", lambda peer: up.at[:, aligned(peer, SLAB), :], lambda me: us.at[:, :, lanes_of(me)]
                )
                c_us = local(up.at[:, my_rows, :], us.at[:, :, lanes_of(r)])
                w_uit()
                vprod[...] = mm(uinvt[TOPL - 1], linvt[TOPL - 1]).astype(BF16)
                known_x = [nt(top_y[n].astype(BF16), uinvt[n]) for n in range(2)]
            if a == 3:
                known_x.append(nt(top_y[2].astype(BF16), uinvt[2]))
                f_ut()
                c_ut.wait()
                w_ut()
                for n, tile in enumerate((0, 1, 0)):
                    nprod[n] = mm(uinvt[n], ut[tile]).astype(BF16)
            await_slot(zr.at[place], slot)
            for m in range(a, TOPL):
                pend[m] = pend[m] + zr[base + m - a].astype(F32)
        low = (top_rhs[a] - pend[a]).astype(BF16)
        if a == 0:
            top_y.append(nt(low, linvt[a]))
            low = top_y[0].astype(BF16)
            for b in range(3):
                pend[b + 1] = pend[b + 1] + nt(low, ltp[b])
        elif a < TOPL - 1:
            for m in range(a + 1, TOPL):
                pend[m] = pend[m] + nt(low, mprod[m - 2 if a == 1 else 2])
            top_y.append(nt(low, linvt[a]))
        else:
            known_x.append(nt(low, vprod[...]))

    tiles = [jnp.zeros((CP, CG), F32) for _ in range(ROWS)]
    for a in reversed(range(TOPL)):
        solved = known_x[a]
        if a < TOPL - 1:
            if a == 2:
                known = [pltpu.roll(tile, SLAB, 1) for tile in tiles]
            else:
                known = tiles
            above = jnp.concatenate(known, axis=-1).astype(BF16)
            solved = solved - nt(above, nprod[a])
        for q in range(2):
            half = solved[:, q * CG:(q + 1) * CG]
            for s in range(4):
                piece = half if a == s else pltpu.roll(half, (a - s) * SLAB % CG, 1)
                tiles[4 * q + s] = jnp.where(slot_of_lane == a, piece, tiles[4 * q + s])
    my_cp = aligned(r, CP)
    xp[my_cp, :] = jnp.concatenate(tiles, axis=-1).astype(BF16)
    w_xp = spread("row", lambda peer: xp.at[my_cp, :], lambda me: xp.at[aligned(me, CP), :])

    lane_slot = lax.shift_right_logical(lax.broadcasted_iota(jnp.int32, (8, CG), 1), 5)
    for j in range(NPL):
        mask = jnp.where(lane_slot == j, 1.0, 0.0).astype(F32)[0:1, :].astype(BF16)
        for q in range(ROWS):
            tree_w[j, :, q * CG:(q + 1) * CG] = ut[2, :, q * CG:(q + 1) * CG] * mask
    c_us.wait()
    w_us()
    w_xp()
    path = xp[...]
    path_term2 = nt(us[NPL:LOC].reshape(NPL * SLAB, ROWS * CG), path)
    for i in range(NPL):
        value = y[NPL + i, my_rows, :] - path_term2[i * SLAB:(i + 1) * SLAB, :]
        sb2[i, my_rows, :] = value.astype(BF16)
    f_sb2, w_sb2 = spread_row_shared(sb2.at[:, my_rows, :], lambda me: sb2.at[:, aligned(me, SLAB), :])
    path_term1 = nt(us[0:NPL].reshape(NPL * SLAB, ROWS * CG), path)
    for j in range(NPL):
        value = y[j, my_rows, :] - path_term1[j * SLAB:(j + 1) * SLAB, :]
        sb1[j, my_rows, :] = value.astype(BF16)
    f_sb1, w_sb1 = spread_row_shared(sb1.at[:, my_rows, :], lambda me: sb1.at[:, aligned(me, SLAB), :])
    own_path = nt(eye, xp[:, lanes_of(r)])
    for m in range(TOPL):
        out_p[m] = own_path[m * SLAB:(m + 1) * SLAB, :]
    piece_rows = SLAB // COLS

    def out_rows(peer):
        return pl.ds(pl.multiple_of(peer * piece_rows, piece_rows), piece_rows)

    w_outp = spread(
        "col", lambda peer: out_p.at[:, out_rows(peer), :], lambda me: x_path.at[0, :, :, lanes_of(me)]
    )
    c_outp = local(out_p.at[:, out_rows(c), :], x_path.at[0, :, :, my_cols])

    w_ui2()
    c_uiown.wait()
    drain(14)

    @pl.when(edge)
    def _():
        for copy in last_sends:
            copy.wait_send()

    f_sb2()
    f_sb1()
    w_sb2()
    for i in range(NPL):
        x2low[i] = mm(uinv2[i], sb2[i]).astype(BF16)
    parent_x = [x2low[parent[j]].reshape(ROWS, 1, SLAB, CG) for j in range(NPL)]
    stacked = jnp.concatenate(parent_x, axis=1).reshape(ROWS * NPL * SLAB, CG)
    trees = [mm(tree_w[j], stacked) for j in range(NPL)]
    for i in range(NPL):
        out_l[NPL + i] = mm(uinv_own[NPL + i], sb2[i])

    def send_out(first):
        part = pl.ds(first, NPL)
        wait = spread(
            "col", lambda peer: out_l.at[part, out_rows(peer), :], lambda me: x_local.at[part, :, lanes_of(me)]
        )
        return wait, local(out_l.at[part, out_rows(c), :], x_local.at[part, :, my_cols])

    w_out2, c_out2 = send_out(NPL)
    w_sb1()
    for j in range(NPL):
        out_l[j] = mm(uinv_own[j], (sb1[j].astype(F32) - trees[j]).astype(BF16))
    w_out1, c_out1 = send_out(0)
    w_outp()
    w_out2()
    c_outp.wait()
    c_out2.wait()
    drain(COLS - 1)
    w_out1()
    c_out1.wait()
    drain()


def per_device(*arrays):
    arrays = list(arrays)
    for index in (4, 5, 6):
        arrays[index] = jnp.swapaxes(arrays[index], -1, -2)
    any_space = pl.BlockSpec(memory_space=pl.ANY)
    vmem = pltpu.VMEM
    scratch = [
        vmem((NPL, SLAB, KCH), BF16),
        vmem((LOC, TOPL, SLAB, KCH), BF16),
        vmem((3, TOPL, SLAB, KCH), BF16),
        vmem((NPL, SLAB, KCH), BF16),
        vmem((LOC, TOPL, SLAB, KCH), BF16),
        vmem((3, TOPL, SLAB, KCH), BF16),
        vmem((LOC, SLAB, W), BF16),
        vmem((NPL, SLAB, CG), BF16),
        vmem((TOPL, SLAB, CG), BF16),
        vmem((NPL, W, CG), BF16),
        vmem((LOC, W, W), BF16),
        vmem((COLS, NPL // 2, SLAB, CG), BF16),
        vmem((COLS, TOPL * SLAB, LOC * KCH), BF16),
        vmem((COLS, 3, SLAB, CG), BF16),
        vmem((6, W, W), BF16),
        vmem((TOPL, W, W), BF16),
        vmem((TOPL, W, W), BF16),
        vmem((NPL, W, W), BF16),
        vmem((LOC, W, CG), BF16),
        vmem((LOC, SLAB, ROWS * CG), BF16),
        vmem((3, W, CG), BF16),
        vmem((3, W, ROWS * CG), BF16),
        vmem((NPL, W, ROWS * CG), BF16),
        vmem((3, W, W), BF16),
        vmem((W, W), BF16),
        vmem((3, W, ROWS * CG), BF16),
        vmem((LOC, W, CG), F32),
        vmem((LOC, W, CG), BF16),
        vmem((NPL, W, CG), BF16),
        vmem((CG, TOPL * SLAB), BF16),
        vmem((2, ROWS, CP, CG), BF16),
        vmem((CG, TOPL * SLAB), BF16),
        vmem((ROWS, CP, CG), BF16),
        vmem((10, CP, W), BF16),
        vmem((10, CP, W), BF16),
        vmem((CG, ROWS * CG), BF16),
        vmem((NPL, W, CG), BF16),
        vmem((NPL, W, CG), BF16),
        vmem((NPL, W, CG), BF16),
        vmem((LOC, SLAB, CG), F32),
        vmem((TOPL, SLAB, CG), F32),
        pltpu.SemaphoreType.DMA((48,)),
        pltpu.SemaphoreType.DMA((200,)),
        pltpu.SemaphoreType.DMA((200,)),
    ]
    return pl.pallas_call(
        kernel,
        out_shape=(
            vmem((LOC, SLAB // COLS, R), F32),
            vmem((1, TOPL, SLAB // COLS, R), F32),
        ),
        in_specs=[pl.BlockSpec(memory_space=pltpu.SMEM)] + [any_space] * 12,
        out_specs=(any_space, any_space),
        scratch_shapes=scratch,
        compiler_params=pltpu.CompilerParams(
            collective_id=0, has_side_effects=True, vmem_limit_bytes=60 * 1024 * 1024
        ),
    )(*arrays)


def solution(mesh):
    placed = (
        P("gz"),
        P("gz", "row", "col"),
        P("gz", None, "row", "col"),
        P(None, None, "row", "col"),
        P("gz", "col", "row"),
        P("gz", None, "col", "row"),
        P(None, None, "col", "row"),
        P("gz", "col", None),
        P(None, "col", None),
        P("gz", "row", None),
        P(None, "row", None),
        P("gz", "row", None),
        P(None, "row", None),
    )
    return jax.shard_map(
        per_device,
        mesh=mesh,
        in_specs=placed,
        out_specs=(P("gz", ("row", "col"), None), P("gz", None, ("row", "col"), None)),
        check_vma=False,
    )
```

```python
import functools

import jax
import jax.numpy as jnp
from jax import lax
from jax.experimental import pallas as pl
from jax.experimental.pallas import tpu as pltpu
from jax.sharding import PartitionSpec as P

F32 = jnp.float32
BF16 = jnp.bfloat16
MESH = pl.DeviceIdType.MESH
ROWS, COLS, LAYERS = 8, 4, 16
NPL, LOC, TOPL = 4, 8, 4
W, R = 256, 512
SLAB, KCH = W // ROWS, W // COLS
CG = R // COLS
CP = CG // ROWS
L_PAIRS = ((0, 1), (0, 2), (0, 3), (1, 2), (1, 3), (2, 3))
Z_BASE = (0, 4, 7, 9)
FAR_FIRST = {8: (4, 3, 5, 2, 6, 1, 7), 4: (2, 1, 3)}


def nt(a, b):
    return lax.dot_general(a, b, (((1,), (1,)), ((), ())), preferred_element_type=F32)


def mm(a, b):
    return jnp.dot(a, b, preferred_element_type=F32)


def aligned(value, size):
    return pl.ds(pl.multiple_of(value * size, size), size)


def kernel(
    parent, l_tree, l_path, l_top, u_tree, u_path, u_top, linv_local, linv_top, uinv_local,
    uinv_top, rhs_local, rhs_top, x_local, x_path,
    st_ltree, st_lpath, st_ltop, st_utree, st_upath, st_utop, uinv_own, rhs2_own, st_rt,
    x1, linv, lt, lp, ltp1, ltp, linvt, uinvt, uinv2, up, us, utp, ut, tree_w, mprod, vprod,
    y, ylow, s2f, tt, rv, rt, rr, zs, zr, xp, sb2, x2low, sb1, out_l, out_p,
    lsem, ssem, rsem,
):
    r = lax.axis_index("row")
    c = lax.axis_index("col")
    g = lax.axis_index("gz")
    chip, core = r // 2, lax.rem(r, 2)
    sibling = chip * 2 + 1 - core
    counters = {"l": 0, "s": 0, "r": 0}
    pending_sends = []

    def take(kind, count=1):
        first = counters[kind]
        counters[kind] += count
        return first

    def local(src, dst):
        copy = pltpu.make_async_copy(src, dst, lsem.at[take("l")])
        copy.start()
        return copy

    def remote(src, dst, slot, target):
        copy = pltpu.make_async_remote_copy(
            src_ref=src, dst_ref=dst, send_sem=ssem.at[take("s")], recv_sem=rsem.at[slot],
            device_id=target, device_id_type=MESH,
        )
        copy.start()
        pending_sends.append(copy)

    def drain(keep=0):
        done = len(pending_sends) - keep
        for copy in pending_sends[:done]:
            copy.wait_send()
        del pending_sends[:done]

    def await_slot(dst, slot):
        pltpu.make_async_remote_copy(
            src_ref=dst, dst_ref=dst, send_sem=ssem.at[0], recv_sem=rsem.at[slot],
            device_id={"row": r}, device_id_type=MESH,
        ).wait_recv()

    def spread(axis, src_of, dst_of):
        me, size = (r, ROWS) if axis == "row" else (c, COLS)
        base = take("r", size)
        for step in FAR_FIRST[size]:
            peer = lax.rem(me + step, size)
            remote(src_of(peer), dst_of(me), base + step, {axis: peer})

        def wait():
            for step in range(1, size):
                await_slot(dst_of(lax.rem(me + size - step, size)), base + step)

        return wait

    def row_of(other_chip, other_core):
        return lax.rem(other_chip + 4, 4) * 2 + other_core

    def spread_row_shared(src, dst_of):
        base = take("r", 8)
        for step in range(1, 4):
            remote(src, dst_of(r), base + step, {"row": row_of(chip + step, core)})
        remote(src, dst_of(r), base, {"row": sibling})

        def forward():
            for step in range(1, 4):
                place = dst_of(row_of(chip - step, core))
                await_slot(place, base + step)
                remote(place, place, base + 4 + step, {"row": sibling})

        def wait():
            await_slot(dst_of(sibling), base)
            for step in range(1, 4):
                await_slot(dst_of(row_of(chip - step, 1 - core)), base + 4 + step)

        return forward, wait

    def spread_col_shared(src, dst_of):
        base = take("r", 8)
        for step in range(1, COLS):
            remote(src, dst_of(c, core), base + step, {"col": lax.rem(c + step, COLS)})

        def forward():
            for step in range(1, COLS):
                place = dst_of(lax.rem(c + COLS - step, COLS), core)
                await_slot(place, base + step)
                remote(place, place, base + 4 + step, {"row": sibling})

        def wait():
            for step in range(1, COLS):
                await_slot(dst_of(lax.rem(c + COLS - step, COLS), 1 - core), base + 4 + step)

        return forward, wait

    anc = [LAYERS - (LAYERS >> a) + g // 2 ** (a + 1) for a in range(TOPL)]
    my_rows = aligned(r, SLAB)
    my_k = aligned(c, KCH)
    my_cols = aligned(c, CG)
    half_src = aligned(core, SLAB)

    def half_rows(owner, half):
        return aligned(owner * 2 + half, SLAB)

    def lanes_of(owner):
        return pl.ds(pl.multiple_of(owner * CG, CG), CG)


    barrier = pltpu.get_barrier_semaphore()

    def greet(target):
        pl.semaphore_signal(barrier, inc=1, device_id=target, device_id_type=MESH)

    partners = []
    for a in range(TOPL - 1):
        span = 2**a
        partners.append(g + span - 2 * span * lax.rem(g // span, 2))
    quarter = g // 4
    source = jnp.where(quarter == 0, 15, jnp.where(quarter == 1, 8, jnp.where(quarter == 2, 7, 0)))
    edge = jnp.logical_or(jnp.logical_or(g == 0, g == 7), jnp.logical_or(g == 8, g == 15))
    far_target = jnp.where(g == 0, 12, jnp.where(g == 7, 11, jnp.where(g == 8, 4, 3)))
    inward = 1 - 2 * lax.rem(g, 2)
    for step in range(1, COLS):
        greet({"col": lax.rem(c + step, COLS)})
    for step in range(1, ROWS):
        greet({"row": lax.rem(r + step, ROWS)})
    greet({"gz": source})
    greet({"gz": partners[2]})
    greet({"gz": partners[1]})
    for step in range(ROWS):
        greet({"row": lax.rem(r + step, ROWS), "gz": partners[0]})

    c_ltree = local(l_tree, st_ltree)
    c_lpath = local(l_path, st_lpath)
    c_ltop = [local(l_top.at[anc[a]], st_ltop.at[a]) for a in range(3)]

    pl.semaphore_wait(barrier, ROWS - 1 + ROWS + COLS - 1 + 2 + jnp.where(edge, 4, 0))

    w_x1 = spread(
        "row", lambda peer: rhs_local.at[pl.ds(0, NPL), :, my_cols],
        lambda me: x1.at[:, aligned(me, SLAB), :],
    )
    f_li1, w_li1 = spread_col_shared(
        linv_local.at[pl.ds(0, NPL), half_src], lambda o, h: linv.at[pl.ds(0, NPL), half_rows(o, h), :]
    )
    c_x1 = local(rhs_local.at[pl.ds(0, NPL), :, my_cols], x1.at[:, my_rows, :])
    c_li1 = local(linv_local.at[pl.ds(0, NPL)], linv.at[pl.ds(0, NPL), my_k, :])
    c_lit = [local(linv_top.at[anc[a]], linvt.at[a, my_k, :]) for a in range(TOPL)]
    c_uit = [local(uinv_top.at[anc[a]], uinvt.at[a, my_rows, :]) for a in range(TOPL)]
    c_rt = [local(rhs_top.at[anc[a], :, my_cols], st_rt.at[a]) for a in range(TOPL)]
    c_li2 = local(linv_local.at[pl.ds(NPL, NPL)], linv.at[pl.ds(NPL, NPL), my_k, :])
    c_rhs2 = local(rhs_local.at[pl.ds(NPL, NPL), :, my_cols], rhs2_own)
    c_utop = [local(u_top.at[anc[a]], st_utop.at[a]) for a in range(3)]
    c_utree = local(u_tree, st_utree)
    c_upath = local(u_path, st_upath)
    c_ui2 = local(uinv_local.at[pl.ds(NPL, NPL)], uinv2.at[:, my_rows, :])
    c_uiown = local(uinv_local, uinv_own)

    c_ltree.wait()
    for b in range(NPL // 2):
        lt[c, b] = jnp.concatenate([st_ltree[2 * b], st_ltree[2 * b + 1]], axis=-1)
    w_lt = spread("col", lambda peer: lt.at[c], lambda me: lt.at[me])
    for copy in c_ltop:
        copy.wait()
    for b in range(len(L_PAIRS) // 2):
        (a1, m1), (a2, m2) = L_PAIRS[2 * b], L_PAIRS[2 * b + 1]
        ltp1[c, b] = jnp.concatenate([st_ltop[a1, m1], st_ltop[a2, m2]], axis=-1)
    w_ltp1a = spread("col", lambda peer: ltp1.at[c, pl.ds(0, 2)], lambda me: ltp1.at[me, pl.ds(0, 2)])
    f_li2, w_li2 = spread_col_shared(
        linv_local.at[pl.ds(NPL, NPL), half_src], lambda o, h: linv.at[pl.ds(NPL, NPL), half_rows(o, h), :]
    )
    c_lpath.wait()
    for m in range(TOPL):
        lp[c, pl.ds(m * SLAB, SLAB), :] = jnp.concatenate([st_lpath[k, m] for k in range(LOC)], axis=-1)
    w_lp = spread("col", lambda peer: lp.at[c], lambda me: lp.at[me])

    def unpaired(pieces, b):
        half = pl.ds(b % 2 * KCH, KCH)
        return jnp.concatenate([pieces[q, b // 2, :, half] for q in range(COLS)], axis=-1)

    for copy in c_lit:
        copy.wait()
    first, rest = pl.ds(0, 1), pl.ds(1, TOPL - 1)
    f_lit0, w_lit0 = spread_col_shared(
        linvt.at[first, half_rows(c, core), :], lambda o, h: linvt.at[first, half_rows(o, h), :]
    )
    w_ltp1b = spread("col", lambda peer: ltp1.at[c, pl.ds(2, 1)], lambda me: ltp1.at[me, pl.ds(2, 1)])
    f_lit, w_lit = spread_col_shared(
        linvt.at[rest, half_rows(c, core), :], lambda o, h: linvt.at[rest, half_rows(o, h), :]
    )
    for copy in c_uit:
        copy.wait()
    f_uit, w_uit = spread_row_shared(uinvt.at[:, my_rows, :], lambda me: uinvt.at[:, aligned(me, SLAB), :])

    c_ui2.wait()
    f_ui2, w_ui2 = spread_row_shared(uinv2.at[:, my_rows, :], lambda me: uinv2.at[:, aligned(me, SLAB), :])

    c_x1.wait()
    c_li1.wait()
    f_li1()
    w_x1()
    w_li1()
    for j in range(NPL):
        solved = mm(linv[j], x1[j])
        y[j] = solved
        ylow[j] = solved.astype(BF16)
    w_lt()
    terms = []
    for j in range(NPL):
        terms.append(mm(unpaired(lt, j), ylow[j]))
    c_rhs2.wait()
    for i in range(NPL):
        value = rhs2_own[i].astype(F32)
        for j in range(NPL):
            value = value - jnp.where(parent[j] == i, 1.0, 0.0).astype(F32) * terms[j]
        s2f[i, my_rows, :] = value.astype(BF16)
    f_s2, w_s2 = spread_row_shared(s2f.at[:, my_rows, :], lambda me: s2f.at[:, aligned(me, SLAB), :])

    eye = (
        lax.broadcasted_iota(jnp.int32, (CG, CG), 0) == lax.broadcasted_iota(jnp.int32, (CG, CG), 1)
    ).astype(F32).astype(BF16)
    for copy in c_rt:
        copy.wait()
    rt[...] = nt(eye, st_rt[...].reshape(TOPL * SLAB, CG)).astype(BF16)
    w_rr = spread("row", lambda peer: rt.at[aligned(peer, CP), :], lambda me: rr.at[me])
    rr[r] = rt[aligned(r, CP), :]
    w_ltp1a()
    for b in range(4):
        ltp[b, my_rows, :] = unpaired(ltp1, b)
    lower, upper = pl.ds(0, 3), pl.ds(3, 3)
    f_ltpa, w_ltpa = spread_row_shared(
        ltp.at[lower, my_rows, :], lambda me: ltp.at[lower, aligned(me, SLAB), :]
    )
    f_li2()

    eye_k = eye[0:KCH, 0:KCH]

    def packed(stack):
        return nt(eye_k, stack).astype(BF16)

    for copy in c_utop:
        copy.wait()
    utp[0, my_k, :] = packed(jnp.concatenate([st_utop[2, 3], st_utop[0, 1], st_utop[0, 2], st_utop[0, 3]], axis=0))
    utp[1, my_k, :] = packed(st_utop[1].reshape(CG, KCH))
    c_utree.wait()
    utp[2, my_k, :] = packed(st_utree[...].reshape(CG, KCH))
    w_utp = spread("col", lambda peer: utp.at[:, my_k, :], lambda me: utp.at[:, aligned(me, KCH), :])
    c_upath.wait()
    for k in range(LOC):
        up[k, my_k, :] = packed(st_upath[k].reshape(CG, KCH))

    w_up = spread("col", lambda peer: up.at[:, my_k, :], lambda me: up.at[:, aligned(me, KCH), :])
    f_s2()
    w_lp()
    toward = jnp.zeros((TOPL * SLAB, CG), F32)
    for q in range(COLS):
        block = ylow[0:NPL, q * KCH:(q + 1) * KCH, :].reshape(NPL * KCH, CG)
        toward = toward + mm(lp[q, :, 0:NPL * KCH], block)

    c_li2.wait()
    w_li2()
    w_s2()
    for i in range(NPL):
        solved = mm(linv[NPL + i], s2f[i])
        y[NPL + i] = solved
        ylow[NPL + i] = solved.astype(BF16)
    for q in range(COLS):
        block = ylow[NPL:LOC, q * KCH:(q + 1) * KCH, :].reshape(NPL * KCH, CG)
        toward = toward + mm(lp[q, :, NPL * KCH:LOC * KCH], block)
    tt[...] = nt(eye, toward.astype(BF16)).astype(BF16)
    base = take("r", 2 * ROWS)
    for step in FAR_FIRST[ROWS]:
        peer = lax.rem(r + step, ROWS)
        remote(tt.at[aligned(peer, CP), :], rv.at[1, r], base + ROWS + step, {"row": peer, "gz": partners[0]})
        remote(tt.at[aligned(peer, CP), :], rv.at[0, r], base + step, {"row": peer})
    remote(tt.at[aligned(r, CP), :], rv.at[1, r], base + ROWS, {"gz": partners[0]})
    rv[0, r] = tt[aligned(r, CP), :]

    def w_rv():
        await_slot(rv.at[1, r], base + ROWS)
        for step in range(1, ROWS):
            sender = lax.rem(r + ROWS - step, ROWS)
            await_slot(rv.at[0, sender], base + step)
            await_slot(rv.at[1, sender], base + ROWS + step)

    f_lit0()
    w_ltp1b()
    for b in range(4, 6):
        ltp[b, my_rows, :] = unpaired(ltp1, b)
    f_ltpb, w_ltpb = spread_row_shared(
        ltp.at[upper, my_rows, :], lambda me: ltp.at[upper, aligned(me, SLAB), :]
    )

    slot_of_lane = lax.shift_right_logical(lax.broadcasted_iota(jnp.int32, (CP, CG), 1), 5)

    def by_level(tiles, m):
        halves = []
        for q in range(2):
            total = None
            for s in range(4):
                piece = tiles[4 * q + s]
                if s != m:
                    piece = pltpu.roll(piece, (s - m) * SLAB % CG, 1)
                total = piece if total is None else jnp.where(slot_of_lane == s, piece, total)
            halves.append(total)
        return jnp.concatenate(halves, axis=-1)

    w_rr()
    rr_tiles = [rr[q].astype(F32) for q in range(ROWS)]
    top_rhs = [by_level(rr_tiles, m) for m in range(TOPL)]
    w_utp()
    f_ut, w_ut = spread_row_shared(utp, lambda me: ut.at[:, :, lanes_of(me)])
    c_ut = local(utp, ut.at[:, :, lanes_of(r)])
    f_ltpa()
    w_rv()
    rv_tiles = [rv[0, q].astype(F32) + rv[1, q].astype(F32) for q in range(ROWS)]
    pend = [by_level(rv_tiles, m) for m in range(TOPL)]
    w_lit0()
    w_ltpa()

    top_y = []
    for a in range(TOPL):
        count = TOPL - a
        base = Z_BASE[a]
        if a > 0:
            place = pl.ds(base, count)
            for m in range(a, TOPL):
                zs[base + m - a] = pend[m].astype(BF16)
            slot = take("r")
            if a < TOPL - 1:
                remote(zs.at[place], zr.at[place], slot, {"gz": partners[a]})
            else:
                last_sends = [
                    pltpu.make_async_remote_copy(
                        src_ref=zs.at[place], dst_ref=zr.at[place], send_sem=ssem.at[take("s")],
                        recv_sem=rsem.at[slot], device_id={"gz": far_target + inward * step}, device_id_type=MESH,
                    )
                    for step in range(4)
                ]

                @pl.when(edge)
                def _():
                    for copy in last_sends:
                        copy.start()

            if a == 1:
                f_lit()
                f_ltpb()
                f_uit()
                f_ui2()
                w_lit()
                w_ltpb()
                for n, (b, below) in enumerate(((3, 1), (4, 1), (5, 2))):
                    mprod[n] = mm(ltp[b], linvt[below]).astype(BF16)
            if a == 2:
                w_up()
                w_us = spread(
                    "row", lambda peer: up.at[:, aligned(peer, SLAB), :], lambda me: us.at[:, :, lanes_of(me)]
                )
                c_us = local(up.at[:, my_rows, :], us.at[:, :, lanes_of(r)])
                w_uit()
                vprod[...] = mm(uinvt[TOPL - 1], linvt[TOPL - 1]).astype(BF16)
                known_x = [nt(top_y[n].astype(BF16), uinvt[n]) for n in range(2)]
            if a == 3:
                known_x.append(nt(top_y[2].astype(BF16), uinvt[2]))
                f_ut()
            await_slot(zr.at[place], slot)
            for m in range(a, TOPL):
                pend[m] = pend[m] + zr[base + m - a].astype(F32)
        low = (top_rhs[a] - pend[a]).astype(BF16)
        if a == 0:
            top_y.append(nt(low, linvt[a]))
            low = top_y[0].astype(BF16)
            for b in range(3):
                pend[b + 1] = pend[b + 1] + nt(low, ltp[b])
        elif a < TOPL - 1:
            for m in range(a + 1, TOPL):
                pend[m] = pend[m] + nt(low, mprod[m - 2 if a == 1 else 2])
            top_y.append(nt(low, linvt[a]))
        else:
            known_x.append(nt(low, vprod[...]))

    c_ut.wait()
    w_ut()
    tiles = [jnp.zeros((CP, CG), F32) for _ in range(ROWS)]
    for a in reversed(range(TOPL)):
        solved = known_x[a]
        if a < TOPL - 1:
            if a == 2:
                known = [pltpu.roll(tile, SLAB, 1) for tile in tiles]
            else:
                known = tiles
            above = jnp.concatenate(known, axis=-1).astype(BF16)
            solved = solved - nt(nt(above, ut[0 if a != 1 else 1]).astype(BF16), uinvt[a])
        for q in range(2):
            half = solved[:, q * CG:(q + 1) * CG]
            for s in range(4):
                piece = half if a == s else pltpu.roll(half, (a - s) * SLAB % CG, 1)
                tiles[4 * q + s] = jnp.where(slot_of_lane == a, piece, tiles[4 * q + s])
    my_cp = aligned(r, CP)
    xp[my_cp, :] = jnp.concatenate(tiles, axis=-1).astype(BF16)
    w_xp = spread("row", lambda peer: xp.at[my_cp, :], lambda me: xp.at[aligned(me, CP), :])

    lane_slot = lax.shift_right_logical(lax.broadcasted_iota(jnp.int32, (8, CG), 1), 5)
    for j in range(NPL):
        mask = jnp.where(lane_slot == j, 1.0, 0.0).astype(F32)[0:1, :].astype(BF16)
        for q in range(ROWS):
            tree_w[j, :, q * CG:(q + 1) * CG] = ut[2, :, q * CG:(q + 1) * CG] * mask
    c_us.wait()
    w_us()
    w_xp()
    path = xp[...]
    path_term2 = nt(us[NPL:LOC].reshape(NPL * SLAB, ROWS * CG), path)
    for i in range(NPL):
        value = y[NPL + i, my_rows, :] - path_term2[i * SLAB:(i + 1) * SLAB, :]
        sb2[i, my_rows, :] = value.astype(BF16)
    f_sb2, w_sb2 = spread_row_shared(sb2.at[:, my_rows, :], lambda me: sb2.at[:, aligned(me, SLAB), :])
    path_term1 = nt(us[0:NPL].reshape(NPL * SLAB, ROWS * CG), path)
    for j in range(NPL):
        value = y[j, my_rows, :] - path_term1[j * SLAB:(j + 1) * SLAB, :]
        sb1[j, my_rows, :] = value.astype(BF16)
    f_sb1, w_sb1 = spread_row_shared(sb1.at[:, my_rows, :], lambda me: sb1.at[:, aligned(me, SLAB), :])
    own_path = nt(eye, xp[:, lanes_of(r)])
    for m in range(TOPL):
        out_p[m] = own_path[m * SLAB:(m + 1) * SLAB, :]
    piece_rows = SLAB // COLS

    def out_rows(peer):
        return pl.ds(pl.multiple_of(peer * piece_rows, piece_rows), piece_rows)

    w_outp = spread(
        "col", lambda peer: out_p.at[:, out_rows(peer), :], lambda me: x_path.at[0, :, :, lanes_of(me)]
    )
    c_outp = local(out_p.at[:, out_rows(c), :], x_path.at[0, :, :, my_cols])

    w_ui2()
    c_uiown.wait()
    drain(14)

    @pl.when(edge)
    def _():
        for copy in last_sends:
            copy.wait_send()

    f_sb2()
    f_sb1()
    w_sb2()
    for i in range(NPL):
        x2low[i] = mm(uinv2[i], sb2[i]).astype(BF16)
    parent_x = [x2low[parent[j]].reshape(ROWS, 1, SLAB, CG) for j in range(NPL)]
    stacked = jnp.concatenate(parent_x, axis=1).reshape(ROWS * NPL * SLAB, CG)
    trees = [mm(tree_w[j], stacked) for j in range(NPL)]
    for i in range(NPL):
        out_l[NPL + i] = mm(uinv_own[NPL + i], sb2[i])

    def send_out(first):
        part = pl.ds(first, NPL)
        wait = spread(
            "col", lambda peer: out_l.at[part, out_rows(peer), :], lambda me: x_local.at[part, :, lanes_of(me)]
        )
        return wait, local(out_l.at[part, out_rows(c), :], x_local.at[part, :, my_cols])

    w_out2, c_out2 = send_out(NPL)
    w_sb1()
    for j in range(NPL):
        out_l[j] = mm(uinv_own[j], (sb1[j].astype(F32) - trees[j]).astype(BF16))
    w_out1, c_out1 = send_out(0)
    w_outp()
    w_out2()
    c_outp.wait()
    c_out2.wait()
    drain(COLS - 1)
    w_out1()
    c_out1.wait()
    drain()


def per_device(*arrays):
    arrays = list(arrays)
    for index in (4, 5, 6):
        arrays[index] = jnp.swapaxes(arrays[index], -1, -2)
    any_space = pl.BlockSpec(memory_space=pl.ANY)
    vmem = pltpu.VMEM
    scratch = [
        vmem((NPL, SLAB, KCH), BF16),
        vmem((LOC, TOPL, SLAB, KCH), BF16),
        vmem((3, TOPL, SLAB, KCH), BF16),
        vmem((NPL, SLAB, KCH), BF16),
        vmem((LOC, TOPL, SLAB, KCH), BF16),
        vmem((3, TOPL, SLAB, KCH), BF16),
        vmem((LOC, SLAB, W), BF16),
        vmem((NPL, SLAB, CG), BF16),
        vmem((TOPL, SLAB, CG), BF16),
        vmem((NPL, W, CG), BF16),
        vmem((LOC, W, W), BF16),
        vmem((COLS, NPL // 2, SLAB, CG), BF16),
        vmem((COLS, TOPL * SLAB, LOC * KCH), BF16),
        vmem((COLS, 3, SLAB, CG), BF16),
        vmem((6, W, W), BF16),
        vmem((TOPL, W, W), BF16),
        vmem((TOPL, W, W), BF16),
        vmem((NPL, W, W), BF16),
        vmem((LOC, W, CG), BF16),
        vmem((LOC, SLAB, ROWS * CG), BF16),
        vmem((3, W, CG), BF16),
        vmem((3, W, ROWS * CG), BF16),
        vmem((NPL, W, ROWS * CG), BF16),
        vmem((3, W, W), BF16),
        vmem((W, W), BF16),
        vmem((LOC, W, CG), F32),
        vmem((LOC, W, CG), BF16),
        vmem((NPL, W, CG), BF16),
        vmem((CG, TOPL * SLAB), BF16),
        vmem((2, ROWS, CP, CG), BF16),
        vmem((CG, TOPL * SLAB), BF16),
        vmem((ROWS, CP, CG), BF16),
        vmem((10, CP, W), BF16),
        vmem((10, CP, W), BF16),
        vmem((CG, ROWS * CG), BF16),
        vmem((NPL, W, CG), BF16),
        vmem((NPL, W, CG), BF16),
        vmem((NPL, W, CG), BF16),
        vmem((LOC, SLAB, CG), F32),
        vmem((TOPL, SLAB, CG), F32),
        pltpu.SemaphoreType.DMA((48,)),
        pltpu.SemaphoreType.DMA((200,)),
        pltpu.SemaphoreType.DMA((200,)),
    ]
    return pl.pallas_call(
        kernel,
        out_shape=(
            vmem((LOC, SLAB // COLS, R), F32),
            vmem((1, TOPL, SLAB // COLS, R), F32),
        ),
        in_specs=[pl.BlockSpec(memory_space=pltpu.SMEM)] + [any_space] * 12,
        out_specs=(any_space, any_space),
        scratch_shapes=scratch,
        compiler_params=pltpu.CompilerParams(
            collective_id=0, has_side_effects=True, vmem_limit_bytes=60 * 1024 * 1024
        ),
    )(*arrays)


def solution(mesh):
    placed = (
        P("gz"),
        P("gz", "row", "col"),
        P("gz", None, "row", "col"),
        P(None, None, "row", "col"),
        P("gz", "col", "row"),
        P("gz", None, "col", "row"),
        P(None, None, "col", "row"),
        P("gz", "col", None),
        P(None, "col", None),
        P("gz", "row", None),
        P(None, "row", None),
        P("gz", "row", None),
        P(None, "row", None),
    )
    return jax.shard_map(
        per_device,
        mesh=mesh,
        in_specs=placed,
        out_specs=(P("gz", ("row", "col"), None), P("gz", None, ("row", "col"), None)),
        check_vma=False,
    )
```
